256 devices in a mesh: seq: 64 (over z_hi, x, y), dp: 4 (over z_lo, core).
Axes of the slice: x: 4, y: 4, z: 8 (z_hi: 4, z_lo: 2; z = z_hi * 2 + z_lo), core: 2. Of those that a mesh axis runs over, the one named last changes fastest.
Arguments:
- query_proj: bfloat16 [8, 512, 8192], P('dp', None, 'seq'), may hold values from -6 to 6
- key_proj: bfloat16 [8, 512, 8192], P('dp', None, 'seq'), may hold values from -6 to 6
- value_proj: bfloat16 [8, 512, 8192], P('dp', None, 'seq'), may hold values from -6 to 6
- long_filter: float32 [512, 8192], P(None, 'seq'), may hold values from -2 to 2
- skip_gain: float32 [512], replicated, may hold values from 0.25 to 1.5
- out_grad: bfloat16 [8, 512, 8192], P('dp', None, 'seq'), may hold values from -6 to 6
Outputs:
- output: bfloat16 [8, 512, 8192], P('dp', None, 'seq')
- grad_query: bfloat16 [8, 512, 8192], P('dp', None, 'seq')
- grad_key: bfloat16 [8, 512, 8192], P('dp', None, 'seq')
- grad_value: bfloat16 [8, 512, 8192], P('dp', None, 'seq')
- grad_filter: float32 [512, 8192], P(None, 'seq')
The draws below stay inside these ranges and needn't reach their ends.
All inputs are finite; a program needn't handle non-finite values.
Results may differ from the reference program's by a relative error of at most 0.0014.
Values sent between devices are 32-bit elements; how exact they have to be, the bound alone decides.
No kernel may reach another device: no remote copies, remote signals or barrier semaphores. Data moves between devices by JAX's collectives and lax.ppermute only.
A program may use at most 64 MiB of HBM per device.

```python
import math
import jax
import jax.numpy as jnp
from jax import lax

G = 512
L = 8192
BATCH = 8


def draw_long_filter(key, part):
    key = jax.random.fold_in(key, 11)
    key_slow, key_fast, key_pick, key_noise = jax.random.split(key, 4)
    slow_rate = jnp.exp(jax.random.uniform(key_slow, (G, 1), jnp.float32, math.log(0.25), math.log(2.3)))
    fast_rate = jnp.exp(jax.random.uniform(key_fast, (G, 1), jnp.float32, math.log(8.0), math.log(L / 40.0)))
    slow_share = 0.5
    pick = jax.random.bernoulli(key_pick, slow_share, (G, 1))
    rate = jnp.where(pick, slow_rate, fast_rate)
    positions = jnp.arange(L, dtype=jnp.float32)[None, :]
    envelope = jnp.exp(-rate * positions / L)
    factor = jnp.sqrt(2.0 * rate / (L * (1.0 - jnp.exp(-2.0 * rate))))
    noise = jnp.clip(jax.random.normal(key_noise, (G, L), jnp.float32), -6.0, 6.0)
    return (noise * envelope * factor).astype(jnp.float32)


def block_levels(own_key, extent, pieces, smallest, top_value):
    factor_of, own = 1.0, jax.random.fold_in(own_key, 6)
    for position, shards_of in pieces:
        heights = jnp.exp(jax.random.uniform(jax.random.fold_in(own, position), (shards_of,), jnp.float32, smallest / len(pieces), top_value / len(pieces)))
        factor_of = factor_of * jnp.repeat(heights, extent[position] // shards_of).reshape([-1 if axis == position else 1 for axis in range(len(extent))])
    return factor_of


def gaussian(key, dims, scale, most, cuts=(), held_as=jnp.bfloat16):
    gain = block_levels(key, dims, cuts, -0.22, 0.18) if cuts else 1.0
    values = jax.random.normal(key, dims, jnp.float32) * scale * gain
    return jnp.minimum(jnp.maximum(values, -most), most).astype(held_as)


def setup_inputs(seed: int = 0) -> dict:
    key_of = jax.random.split(jax.random.key(seed), 7)
    query_proj = gaussian(key_of[0], (BATCH, G, L), 1.0, 6.0, ((0, 4), (2, 64)))
    key_proj = gaussian(key_of[1], (BATCH, G, L), 1.0, 6.0, ((0, 4), (2, 64)))
    value_proj = gaussian(key_of[2], (BATCH, G, L), 1.0, 6.0, ((0, 4), (2, 64)))
    long_filter = draw_long_filter(jax.random.fold_in(key_of[6], 71), 0)
    skip_gain = jnp.clip(jax.random.uniform(key_of[4], (G,), jnp.float32, 0.25, 1.5), 0.25, 1.5)
    out_grad = gaussian(key_of[5], (BATCH, G, L), 1.0, 6.0, ((0, 4), (2, 64)))
    return {"query_proj": query_proj, "key_proj": key_proj, "value_proj": value_proj, "long_filter": long_filter, "skip_gain": skip_gain, "out_grad": out_grad}


def reference(query_proj, key_proj, value_proj, long_filter, skip_gain, out_grad):
    query = query_proj.astype(jnp.float32)
    keys_in = key_proj.astype(jnp.float32)
    values_in = value_proj.astype(jnp.float32)
    upstream = out_grad.astype(jnp.float32)
    padded_len = 2 * L
    mixed_in = keys_in * values_in
    filter_spec = jnp.fft.rfft(long_filter, n=padded_len, axis=-1)
    mixed_spec = jnp.fft.rfft(mixed_in, n=padded_len, axis=-1)
    conv_out = jnp.fft.irfft(mixed_spec * filter_spec[None], n=padded_len, axis=-1)[..., :L].astype(jnp.float32)
    gated_conv = conv_out + skip_gain[None, :, None] * mixed_in
    output = (query * gated_conv).astype(jnp.bfloat16)
    weighted = upstream * query
    weighted_spec = jnp.fft.rfft(weighted, n=padded_len, axis=-1)
    back_conv = jnp.fft.irfft(weighted_spec * jnp.conj(filter_spec)[None], n=padded_len, axis=-1)[..., :L].astype(jnp.float32)
    back_conv = back_conv + skip_gain[None, :, None] * weighted
    grad_query = (upstream * gated_conv).astype(jnp.bfloat16)
    grad_key = (back_conv * values_in).astype(jnp.bfloat16)
    grad_value = (back_conv * keys_in).astype(jnp.bfloat16)
    cross_spec = lax.optimization_barrier(jnp.sum(weighted_spec * jnp.conj(mixed_spec), axis=0))
    filter_terms = jnp.fft.irfft(cross_spec, n=padded_len, axis=-1)[:, :L].astype(jnp.float32)
    grad_filter = filter_terms / jnp.sqrt(jnp.float32(BATCH * L))
    return (output, grad_query, grad_key, grad_value, grad_filter)
```

```python
import math

import jax
import jax.numpy as jnp
import numpy as np
from jax import lax
from jax.experimental import pallas as pl
from jax.experimental.pallas import tpu as pltpu
from jax.sharding import PartitionSpec as P

F32 = jnp.float32
BF16 = jnp.bfloat16
LANES = 128


def split_np(table):
    high = table.astype(jnp.bfloat16)
    low = (table - high.astype(np.float64)).astype(jnp.bfloat16)
    return high, low


def build_tables(half, scale_batch):
    K1 = 2 * half
    total = K1 * LANES
    k1 = np.arange(K1)[:, None]
    n1 = np.arange(half)[None, :]
    ang = 2.0 * np.pi * ((k1 * n1) % K1) / K1
    c1, s1 = np.cos(ang), np.sin(ang)
    enter = np.concatenate(
        [np.concatenate([c1, s1], 1), np.concatenate([-s1, c1], 1)], 0
    )
    enter_real = np.concatenate([c1, -s1], 0)
    n2 = np.arange(LANES)[:, None]
    k2 = np.arange(LANES)[None, :]
    ang2 = 2.0 * np.pi * ((n2 * k2) % LANES) / LANES
    c2, s2 = np.cos(ang2), np.sin(ang2)
    lane_fwd = np.concatenate(
        [np.concatenate([c2, -s2], 1), np.concatenate([s2, c2], 1)], 0
    )
    lane_inv = np.concatenate(
        [np.concatenate([c2, s2], 1), np.concatenate([-s2, c2], 1)], 0
    )
    leave = (
        np.concatenate(
            [np.concatenate([c1.T, -s1.T], 1), np.concatenate([s1.T, c1.T], 1)], 0
        )
        / total
    )
    leave_real = leave[:half] * scale_batch
    angt = 2.0 * np.pi * ((np.arange(K1)[:, None] * np.arange(LANES)[None, :]) % total) / total
    turn = np.concatenate([np.cos(angt), np.sin(angt)], 1).astype(np.float32)

    def dup(table):
        high, low = split_np(table)
        return np.concatenate([high, high], 1), low

    return {
        "enter": dup(enter),
        "enter_real": dup(enter_real),
        "lane_fwd": split_np(lane_fwd),
        "lane_inv": split_np(lane_inv),
        "leave": split_np(leave),
        "leave_real": split_np(leave_real),
        "turn": turn,
    }


def split(value):
    high = value.astype(BF16)
    low = (value - high.astype(F32)).astype(BF16)
    return high, low


def mm(a, b):
    return jnp.dot(a, b, preferred_element_type=F32)


def enter_product(twice_high, low, data):
    high_d, low_d = split(data)
    return mm(twice_high, jnp.concatenate([high_d, low_d], 0)) + mm(low, high_d)


def lane_product(data, high, low):
    rows = data.shape[0]
    high_d, low_d = split(data)
    both = mm(jnp.concatenate([high_d, low_d], 0), high)
    return both[:rows] + both[rows:] + mm(high_d, low)


def leave_product(high, low, data):
    cols = data.shape[1]
    high_d, low_d = split(data)
    both = mm(high, jnp.concatenate([high_d, low_d], 1))
    return both[:, :cols] + both[:, cols:] + mm(low, high_d)


def pre_kernel(devices, rows, dp_ref, q_ref, k_ref, v_ref, g_ref, f_ref, send_ref, hold_ref):
    batch = q_ref.shape[0]
    own = q_ref.shape[1] // devices
    place = 0
    for left, right in ((k_ref, v_ref), (g_ref, q_ref)):
        for b in range(batch):
            hold_ref[...] = left[b].astype(F32) * right[b].astype(F32)
            for c in range(own):
                send_ref[pl.ds(place + c, devices, stride=rows), :] = hold_ref[
                    pl.ds(c, devices, stride=own), :
                ]
            place += own
    extra = rows - place
    d = dp_ref[0]
    for j in range(extra):
        send_ref[pl.ds(place + j, devices, stride=rows), :] = f_ref[
            pl.ds(d * extra + j, devices, stride=own), :
        ]


def twist_forward(part, turn_cos, turn_sin):
    half = part.shape[0] // 2
    re, im = part[:half], part[half:]
    return jnp.concatenate(
        [re * turn_cos + im * turn_sin, im * turn_cos - re * turn_sin], 1
    )


def twist_back(part, turn_cos, turn_sin):
    re, im = part[:, :LANES], part[:, LANES:]
    return jnp.concatenate(
        [re * turn_cos - im * turn_sin, im * turn_cos + re * turn_sin], 0
    )


def front_kernel(
    devices, rows, own, extra, dp_ref, r_ref, enter2, enter_lo, fwd_hi, fwd_lo, inv_hi, inv_lo,
    leave_hi, leave_lo, turn_ref, spec_ref, grad_ref,
):
    step = pl.program_id(0)
    turn_cos, turn_sin = turn_ref[:, :LANES], turn_ref[:, LANES:]
    K1 = 2 * devices
    pieces = []
    for j in range(extra):
        c = step * extra + j
        for sig in range(2):
            base = sig * 2 * own + c
            re = r_ref[pl.ds(base, devices, stride=rows), :]
            im = r_ref[pl.ds(base + own, devices, stride=rows), :]
            pieces.append(jnp.concatenate([re, im], 0))
    data = jnp.concatenate(pieces, 1)
    mid = enter_product(enter2[...], enter_lo[...], data)
    turned = [
        twist_forward(mid[:, i * LANES : (i + 1) * LANES], turn_cos, turn_sin)
        for i in range(2 * extra)
    ]
    spec = lane_product(jnp.concatenate(turned, 0), fwd_hi[...], fwd_lo[...])
    cross = []
    for j in range(extra):
        mixed = spec[(2 * j) * K1 : (2 * j + 1) * K1]
        weighted = spec[(2 * j + 1) * K1 : (2 * j + 2) * K1]
        spec_ref[j, 0] = mixed
        spec_ref[j, 1] = weighted
        mr, mi = mixed[:, :LANES], mixed[:, LANES:]
        wr, wi = weighted[:, :LANES], weighted[:, LANES:]
        cross.append(jnp.concatenate([wr * mr + wi * mi, wi * mr - wr * mi], 1))
    back = lane_product(jnp.concatenate(cross, 0), inv_hi[...], inv_lo[...])
    turned = [
        twist_back(back[j * K1 : (j + 1) * K1], turn_cos, turn_sin) for j in range(extra)
    ]
    final = leave_product(leave_hi[...], leave_lo[...], jnp.concatenate(turned, 1))
    for j in range(extra):
        grad_ref[0, j] = final[:, j * LANES : (j + 1) * LANES]


def back_kernel(
    devices, rows, own, extra, dp_ref, spec_ref, p0, p1, p2, p3, enter2, enter_lo, fwd_hi, fwd_lo,
    inv_hi, inv_lo, leave_hi, leave_lo, turn_ref, send_ref, taps_ref,
):
    step = pl.program_id(0)
    groups = own // extra
    turn_cos, turn_sin = turn_ref[:, :LANES], turn_ref[:, LANES:]
    K1 = 2 * devices
    span = devices * extra

    @pl.when(step == 0)
    def _():
        for i, part in enumerate((p0, p1, p2, p3)):
            taps_ref[pl.ds(i * span, span), :] = part[...]

    pieces = [
        taps_ref[pl.ds(step * span + j, devices, stride=extra), :] for j in range(extra)
    ]
    mid = enter_product(enter2[...], enter_lo[...], jnp.concatenate(pieces, 1))
    turned = [
        twist_forward(mid[:, j * LANES : (j + 1) * LANES], turn_cos, turn_sin)
        for j in range(extra)
    ]
    taps = lane_product(jnp.concatenate(turned, 0), fwd_hi[...], fwd_lo[...])
    products = []
    for j in range(extra):
        hr = taps[j * K1 : (j + 1) * K1, :LANES]
        hi = taps[j * K1 : (j + 1) * K1, LANES:]
        mr, mi = spec_ref[j, 0, :, :LANES], spec_ref[j, 0, :, LANES:]
        wr, wi = spec_ref[j, 1, :, :LANES], spec_ref[j, 1, :, LANES:]
        products.append(jnp.concatenate([mr * hr - mi * hi, mr * hi + mi * hr], 1))
        products.append(jnp.concatenate([wr * hr + wi * hi, wi * hr - wr * hi], 1))
    back = lane_product(jnp.concatenate(products, 0), inv_hi[...], inv_lo[...])
    turned = [
        twist_back(back[i * K1 : (i + 1) * K1], turn_cos, turn_sin) for i in range(2 * extra)
    ]
    final = leave_product(leave_hi[...], leave_lo[...], jnp.concatenate(turned, 1))
    group = lax.rem(dp_ref[0] - step + groups, groups)
    for j in range(extra):
        c = group * extra + j
        for sig in range(2):
            col = (2 * j + sig) * LANES
            for b in range(2):
                send_ref[pl.ds((2 * sig + b) * own + c, devices, stride=rows), :] = final[
                    b * devices : (b + 1) * devices, col : col + LANES
                ]


def post_kernel(
    devices, rows, r_ref, skip_ref, q_ref, k_ref, v_ref, g_ref, out_ref, gq_ref, gk_ref, gv_ref,
    conv_ref, back_ref,
):
    batch, chans = q_ref.shape[0], q_ref.shape[1]
    own = chans // devices
    for b in range(batch):
        for c in range(own):
            conv_ref[pl.ds(c, devices, stride=own), :] = r_ref[
                pl.ds(b * own + c, devices, stride=rows), :
            ]
            back_ref[pl.ds(c, devices, stride=own), :] = r_ref[
                pl.ds((batch + b) * own + c, devices, stride=rows), :
            ]
        skip = skip_ref[...]
        query, keys = q_ref[b].astype(F32), k_ref[b].astype(F32)
        values, upstream = v_ref[b].astype(F32), g_ref[b].astype(F32)
        gated = conv_ref[...] + skip * (keys * values)
        back = back_ref[...] + skip * (upstream * query)
        out_ref[b] = (query * gated).astype(BF16)
        gq_ref[b] = (upstream * gated).astype(BF16)
        gk_ref[b] = (back * values).astype(BF16)
        gv_ref[b] = (back * keys).astype(BF16)


def join_kernel(devices, extra, own, dp_ref, p0, p1, p2, p3, out_ref):
    groups = own // extra
    for i, part in enumerate((p0, p1, p2, p3)):
        group = lax.rem(dp_ref[0] - i + groups, groups)
        for j in range(extra):
            out_ref[pl.ds(group * extra + j, devices, stride=own), :] = part[
                pl.ds(j, devices, stride=extra), :
            ]


VMEM = pl.BlockSpec(memory_space=pltpu.VMEM)
SMEM = pl.BlockSpec(memory_space=pltpu.SMEM)


def whole(array):
    dims = array.ndim
    return pl.BlockSpec(array.shape, lambda i, d: (0,) * dims)


def shards(devices, groups, tables, query_proj, key_proj, value_proj, long_filter, skip_gain, out_grad):
    batch, chans, cols = query_proj.shape
    own = chans // devices
    extra = own // groups
    rows = 2 * batch * own + extra
    K1 = 2 * devices
    place = lax.axis_index("dp").astype(jnp.int32).reshape(1)
    params = pltpu.CompilerParams(vmem_limit_bytes=48 * 1024 * 1024)

    def cost(flops, size):
        return pl.CostEstimate(flops=flops, bytes_accessed=size, transcendentals=0)

    def gather(part):
        parts = [part]
        for k in range(1, groups):
            pairs = [(i, (i + k) % groups) for i in range(groups)]
            parts.append(lax.ppermute(part, "dp", pairs))
        return parts

    def exchange(flat):
        shaped = flat.reshape(devices, rows // 2, 2, cols)
        return lax.all_to_all(shaped, "seq", split_axis=0, concat_axis=0, tiled=True)

    with jax.named_scope("pre"):
        send = pl.pallas_call(
            lambda *refs: pre_kernel(devices, rows, *refs),
            out_shape=jax.ShapeDtypeStruct((devices * rows, cols), F32),
            in_specs=[SMEM] + [VMEM] * 5,
            out_specs=VMEM,
            scratch_shapes=[pltpu.VMEM((chans, cols), F32)],
            compiler_params=params,
            cost_estimate=cost(10**6, 3 * 10**6),
        )(place, query_proj, key_proj, value_proj, out_grad, long_filter)
    with jax.named_scope("out"):
        arrived = exchange(send)
    signals = arrived.reshape(devices * rows, cols)
    with jax.named_scope("taps"):
        own_taps = arrived[:, rows // 2 - extra // 2 :].reshape(devices * extra, cols)
        taps = gather(own_taps)
    T = tables
    front_tables = (*T["enter"], *T["lane_fwd"], *T["lane_inv"], *T["leave_real"], T["turn"])
    with jax.named_scope("front"):
        spec, partial = pl.pallas_call(
            lambda *refs: front_kernel(devices, rows, own, extra, *refs),
            out_shape=[
                jax.ShapeDtypeStruct((own, 2, K1, 2 * cols), F32),
                jax.ShapeDtypeStruct((groups, extra, devices, cols), F32),
            ],
            grid_spec=pltpu.PrefetchScalarGridSpec(
                num_scalar_prefetch=1,
                grid=(groups,),
                in_specs=[whole(signals)] + [whole(t) for t in front_tables],
                out_specs=[
                    pl.BlockSpec((extra, 2, K1, 2 * cols), lambda i, d: (i, 0, 0, 0)),
                    pl.BlockSpec(
                        (1, extra, devices, cols),
                        lambda i, d: (lax.rem(i - d[0] + groups, groups), 0, 0, 0),
                    ),
                ],
            ),
            compiler_params=params,
            cost_estimate=cost(4 * 10**9, 4 * 10**6),
        )(place, signals, *front_tables)
    with jax.named_scope("terms"):
        total = partial[0]
        for k in range(1, groups):
            pairs = [(i, (i + k) % groups) for i in range(groups)]
            total = total + lax.ppermute(partial[k], "dp", pairs)
    back_tables = (*T["enter_real"], *T["lane_fwd"], *T["lane_inv"], *T["leave"], T["turn"])
    with jax.named_scope("back"):
        send = pl.pallas_call(
            lambda *refs: back_kernel(devices, rows, own, extra, *refs),
            out_shape=jax.ShapeDtypeStruct((devices * rows, cols), F32),
            grid_spec=pltpu.PrefetchScalarGridSpec(
                num_scalar_prefetch=1,
                grid=(groups,),
                in_specs=[
                    pl.BlockSpec(
                        (extra, 2, K1, 2 * cols),
                        lambda i, d: (lax.rem(d[0] - i + groups, groups), 0, 0, 0),
                    )
                ]
                + [whole(t) for t in taps]
                + [whole(t) for t in back_tables],
                out_specs=pl.BlockSpec((devices * rows, cols), lambda i, d: (0, 0)),
                scratch_shapes=[pltpu.VMEM((groups * extra * devices, cols), F32)],
            ),
            compiler_params=params,
            cost_estimate=cost(4 * 10**9, 4 * 10**6),
        )(place, spec, *taps, *back_tables)
    with jax.named_scope("return"):
        shaped = send.reshape(devices, rows // 2, 2, cols)
        merged = total.transpose(1, 0, 2).reshape(devices, extra // 2, 2, cols)
        shaped = lax.dynamic_update_slice(shaped, merged, (0, rows // 2 - extra // 2, 0, 0))
        returned = lax.all_to_all(shaped, "seq", split_axis=0, concat_axis=0, tiled=True)
    flat = returned.reshape(devices * rows, cols)
    with jax.named_scope("terms_out"):
        own_terms = returned[:, rows // 2 - extra // 2 :].reshape(devices * extra, cols)
        terms = gather(own_terms)
    with jax.named_scope("post"):
        output, grad_query, grad_key, grad_value = pl.pallas_call(
            lambda *refs: post_kernel(devices, rows, *refs),
            out_shape=[jax.ShapeDtypeStruct((batch, chans, cols), BF16)] * 4,
            in_specs=[VMEM] * 6,
            out_specs=[VMEM] * 4,
            scratch_shapes=[pltpu.VMEM((chans, cols), F32)] * 2,
            compiler_params=params,
            cost_estimate=cost(10**6, 4 * 10**6),
        )(flat, skip_gain[:, None], query_proj, key_proj, value_proj, out_grad)
    with jax.named_scope("join"):
        grad_filter = pl.pallas_call(
            lambda *refs: join_kernel(devices, extra, own, *refs),
            out_shape=jax.ShapeDtypeStruct((chans, cols), F32),
            in_specs=[SMEM] + [VMEM] * 4,
            out_specs=VMEM,
            compiler_params=params,
            cost_estimate=cost(10**5, 5 * 10**5),
        )(place, *terms)
    return (output, grad_query, grad_key, grad_value, grad_filter)


def solution(mesh):
    devices, groups = mesh.shape["seq"], mesh.shape["dp"]
    tables = build_tables(devices, 1.0 / math.sqrt(2 * groups * devices * LANES))

    def run(*args):
        return shards(devices, groups, tables, *args)

    wide = P("dp", None, "seq")
    return jax.shard_map(
        run,
        mesh=mesh,
        in_specs=(wide, wide, wide, P(None, "seq"), P(), wide),
        out_specs=(wide, wide, wide, wide, P(None, "seq")),
        check_vma=False,
    )
```

```python
import math

import jax
import jax.numpy as jnp
import numpy as np
from jax import lax
from jax.experimental import pallas as pl
from jax.experimental.pallas import tpu as pltpu
from jax.sharding import PartitionSpec as P

F32 = jnp.float32
BF16 = jnp.bfloat16
LANES = 128


def split_np(table):
    high = table.astype(jnp.bfloat16)
    low = (table - high.astype(np.float64)).astype(jnp.bfloat16)
    return high, low


def build_tables(half, scale):
    K1 = 2 * half
    total = K1 * LANES
    k1 = np.arange(K1)[:, None]
    n1 = np.arange(half)[None, :]
    ang = 2.0 * np.pi * ((k1 * n1) % K1) / K1
    c1, s1 = np.cos(ang), np.sin(ang)
    enter = np.block([[c1, s1], [-s1, c1]])
    enter_real = np.concatenate([c1, -s1], 0)
    n2 = np.arange(LANES)[:, None]
    k2 = np.arange(LANES)[None, :]
    ang2 = 2.0 * np.pi * ((n2 * k2) % LANES) / LANES
    c2, s2 = np.cos(ang2), np.sin(ang2)
    lane_fwd = np.block([[c2, -s2], [s2, c2]])
    lane_inv = np.block([[c2, s2], [-s2, c2]])
    leave = np.block([[c1.T, -s1.T], [s1.T, c1.T]]) / total
    leave_real = leave[:half] * scale
    phase = (np.arange(K1)[:, None] * np.arange(LANES)[None, :]) % total
    angt = 2.0 * np.pi * phase / total
    turn = np.concatenate([np.cos(angt), np.sin(angt)], 1).astype(np.float32)

    def left(table):
        high, low = split_np(table)
        return np.concatenate([high, high, low], 1)

    def right(table):
        high, low = split_np(table)
        return np.concatenate([high, high, low], 0)

    return (
        left(enter), left(enter_real), right(lane_fwd), right(lane_inv),
        left(leave), left(leave_real), turn,
    )


def parts(value, axis):
    high = value.astype(BF16)
    low = (value - high.astype(F32)).astype(BF16)
    return jnp.concatenate([high, low, high], axis)


def mm(a, b):
    return jnp.dot(a, b, preferred_element_type=F32)


def twist_forward(part, turn_cos, turn_sin):
    half = part.shape[0] // 2
    re, im = part[:half], part[half:]
    return jnp.concatenate(
        [re * turn_cos + im * turn_sin, im * turn_cos - re * turn_sin], 1
    )


def twist_back(part, turn_cos, turn_sin):
    re, im = part[:, :LANES], part[:, LANES:]
    return jnp.concatenate(
        [re * turn_cos - im * turn_sin, im * turn_cos + re * turn_sin], 0
    )


def pre_kernel(
    rows, own, core_ref, q_hbm, k_hbm, v_hbm, g_hbm, f_hbm, send_ref, q, k, v, g, f, hold, sems
):
    batch, chans = q.shape[0], q.shape[1]
    peers = chans // own
    copies = []
    for b in range(batch):
        for i, (src, dst) in enumerate(((k_hbm, k), (v_hbm, v), (g_hbm, g), (q_hbm, q))):
            copies.append(pltpu.make_async_copy(src.at[b], dst.at[b], sems.at[4 * b + i]))
    taps = pltpu.make_async_copy(f_hbm, f, sems.at[4 * batch])
    for copy in copies:
        copy.start()
    taps.start()
    for b in range(batch):
        for sig, (left, right) in enumerate(((k, v), (g, q))):
            copies[4 * b + 2 * sig].wait()
            copies[4 * b + 2 * sig + 1].wait()
            slot = hold.at[2 * b + sig]
            slot[...] = left[b].astype(F32) * right[b].astype(F32)
            for j in range(own):
                send_ref[pl.ds((sig * batch + b) * own + j, peers, stride=rows), :] = slot[
                    pl.ds(j, peers, stride=own), :
                ]
    taps.wait()
    send_ref[pl.ds(2 * batch * own, peers, stride=rows), :] = f[
        pl.ds(core_ref[0], peers, stride=own), :
    ]


def mid_kernel(
    devices, groups, own, batch, rows_in, rows_out, r_ref, enter, enter_real, lane_fwd, lane_inv,
    leave, leave_real, turn_ref, send_ref,
):
    turn_cos, turn_sin = turn_ref[:, :LANES], turn_ref[:, LANES:]
    K1 = 2 * devices
    pairs = 2 * groups
    for j in range(own):
        pieces = []
        for sig in range(2):
            for d in range(groups):
                base = d * rows_in + sig * batch * own + j
                re = r_ref[pl.ds(base, devices, stride=groups * rows_in), :]
                im = r_ref[pl.ds(base + own, devices, stride=groups * rows_in), :]
                pieces.append(jnp.concatenate([re, im], 0))
        taps = r_ref[
            pl.ds(j * rows_in + 2 * batch * own, devices, stride=groups * rows_in), :
        ]
        mid = mm(enter[...], parts(jnp.concatenate(pieces, 1), 0))
        turned = [
            twist_forward(mid[:, i * LANES : (i + 1) * LANES], turn_cos, turn_sin)
            for i in range(pairs)
        ]
        turned.append(twist_forward(mm(enter_real[...], parts(taps, 0)), turn_cos, turn_sin))
        spec = mm(parts(jnp.concatenate(turned, 0), 1), lane_fwd[...])
        hr, hi = spec[pairs * K1 :, :LANES], spec[pairs * K1 :, LANES:]
        products, backs = [], []
        cross_re = cross_im = 0.0
        for d in range(groups):
            mr, mi = spec[d * K1 : (d + 1) * K1, :LANES], spec[d * K1 : (d + 1) * K1, LANES:]
            at = (groups + d) * K1
            wr, wi = spec[at : at + K1, :LANES], spec[at : at + K1, LANES:]
            products.append(jnp.concatenate([mr * hr - mi * hi, mr * hi + mi * hr], 1))
            backs.append(jnp.concatenate([wr * hr + wi * hi, wi * hr - wr * hi], 1))
            cross_re = cross_re + (wr * mr + wi * mi)
            cross_im = cross_im + (wi * mr - wr * mi)
        cross = jnp.concatenate([cross_re, cross_im], 1)
        back = mm(parts(jnp.concatenate(products + backs + [cross], 0), 1), lane_inv[...])
        turned = [
            twist_back(back[i * K1 : (i + 1) * K1], turn_cos, turn_sin)
            for i in range(pairs + 1)
        ]
        final = mm(leave[...], parts(jnp.concatenate(turned[:pairs], 1), 0))
        terms = mm(leave_real[...], parts(turned[pairs], 0))
        for sig in range(2):
            for d in range(groups):
                col = (sig * groups + d) * LANES
                for b in range(batch):
                    base = d * rows_out + (sig * batch + b) * own + j
                    send_ref[pl.ds(base, devices, stride=groups * rows_out), :] = final[
                        b * devices : (b + 1) * devices, col : col + LANES
                    ]
        for d in range(groups):
            base = d * rows_out + 2 * batch * own + j
            send_ref[pl.ds(base, devices, stride=groups * rows_out), :] = terms


def post_kernel(
    rows, own, r_ref, skip_ref, q_ref, k_ref, v_ref, g_ref, out_ref, gq_ref, gk_ref, gv_ref,
    gf_ref, conv_ref, back_ref,
):
    batch, chans = q_ref.shape[0], q_ref.shape[1]
    peers = chans // own
    for j in range(own):
        gf_ref[pl.ds(j, peers, stride=own), :] = r_ref[
            pl.ds(2 * batch * own + j, peers, stride=rows), :
        ]
    skip = skip_ref[...]
    for b in range(batch):
        for j in range(own):
            conv_ref[pl.ds(j, peers, stride=own), :] = r_ref[
                pl.ds(b * own + j, peers, stride=rows), :
            ]
            back_ref[pl.ds(j, peers, stride=own), :] = r_ref[
                pl.ds((batch + b) * own + j, peers, stride=rows), :
            ]
        query, keys = q_ref[b].astype(F32), k_ref[b].astype(F32)
        values, upstream = v_ref[b].astype(F32), g_ref[b].astype(F32)
        gated = conv_ref[...] + skip * (keys * values)
        back = back_ref[...] + skip * (upstream * query)
        out_ref[b] = (query * gated).astype(BF16)
        gq_ref[b] = (upstream * gated).astype(BF16)
        gk_ref[b] = (back * values).astype(BF16)
        gv_ref[b] = (back * keys).astype(BF16)


VMEM = pl.BlockSpec(memory_space=pltpu.VMEM)
SMEM = pl.BlockSpec(memory_space=pltpu.SMEM)
HBM = pl.BlockSpec(memory_space=pltpu.HBM)
MIB = 1024 * 1024


def shards(devices, groups, tables, query_proj, key_proj, value_proj, long_filter, skip_gain, out_grad):
    batch, chans, cols = query_proj.shape
    peers = devices * groups
    own = chans // peers
    rows_in = 2 * batch * own + 1
    rows_out = 2 * batch * own + own
    core = lax.rem(lax.axis_index("dp"), own).astype(jnp.int32).reshape(1)

    def params(mib):
        return pltpu.CompilerParams(vmem_limit_bytes=mib * MIB)

    def exchange(flat, rows):
        shaped = flat.reshape(peers, rows, 1, cols)
        moved = lax.all_to_all(shaped, ("seq", "dp"), split_axis=0, concat_axis=0, tiled=True)
        return moved.reshape(peers * rows, cols)

    with jax.named_scope("pre"):
        wide = pltpu.VMEM((batch, chans, cols), BF16)
        send = pl.pallas_call(
            lambda *refs: pre_kernel(rows_in, own, *refs),
            out_shape=jax.ShapeDtypeStruct((peers * rows_in, cols), F32),
            in_specs=[SMEM] + [HBM] * 5,
            out_specs=VMEM,
            scratch_shapes=[
                wide, wide, wide, wide,
                pltpu.VMEM((chans, cols), F32),
                pltpu.VMEM((2 * batch, chans, cols), F32),
                pltpu.SemaphoreType.DMA((4 * batch + 1,)),
            ],
            compiler_params=params(48),
        )(core, query_proj, key_proj, value_proj, out_grad, long_filter)
    with jax.named_scope("gather"):
        arrived = exchange(send, rows_in)
    with jax.named_scope("mid"):
        send = pl.pallas_call(
            lambda *refs: mid_kernel(devices, groups, own, batch, rows_in, rows_out, *refs),
            out_shape=jax.ShapeDtypeStruct((peers * rows_out, cols), F32),
            in_specs=[VMEM] * (1 + len(tables)),
            out_specs=VMEM,
            compiler_params=params(48),
        )(arrived, *tables)
    with jax.named_scope("scatter"):
        returned = exchange(send, rows_out)
    with jax.named_scope("post"):
        plane = jax.ShapeDtypeStruct((batch, chans, cols), BF16)
        return pl.pallas_call(
            lambda *refs: post_kernel(rows_out, own, *refs),
            out_shape=[plane] * 4 + [jax.ShapeDtypeStruct((chans, cols), F32)],
            in_specs=[VMEM] * 6,
            out_specs=[VMEM] * 5,
            scratch_shapes=[pltpu.VMEM((chans, cols), F32)] * 2,
            compiler_params=params(48),
        )(returned, skip_gain[:, None], query_proj, key_proj, value_proj, out_grad)


def solution(mesh):
    devices, groups = mesh.shape["seq"], mesh.shape["dp"]
    tables = build_tables(devices, 1.0 / math.sqrt(2 * groups * devices * LANES))

    def run(*args):
        return tuple(shards(devices, groups, tables, *args))

    wide = P("dp", None, "seq")
    return jax.shard_map(
        run,
        mesh=mesh,
        in_specs=(wide, wide, wide, P(None, "seq"), P(), wide),
        out_specs=(wide, wide, wide, wide, P(None, "seq")),
        check_vma=False,
    )
```

```python
import math

import jax
import jax.numpy as jnp
import numpy as np
from jax import lax
from jax.experimental import pallas as pl
from jax.experimental.pallas import tpu as pltpu
from jax.sharding import PartitionSpec as P

F32 = jnp.float32
BF16 = jnp.bfloat16
LANES = 128


def split_np(table):
    high = table.astype(jnp.bfloat16)
    low = (table - high.astype(np.float64)).astype(jnp.bfloat16)
    return high, low


def build_tables(half, scale):
    K1 = 2 * half
    total = K1 * LANES
    k1 = np.arange(K1)[:, None]
    n1 = np.arange(half)[None, :]
    ang = 2.0 * np.pi * ((k1 * n1) % K1) / K1
    c1, s1 = np.cos(ang), np.sin(ang)
    enter = np.block([[c1, s1], [-s1, c1]])
    enter_real = np.concatenate([c1, -s1], 0)
    n2 = np.arange(LANES)[:, None]
    k2 = np.arange(LANES)[None, :]
    ang2 = 2.0 * np.pi * ((n2 * k2) % LANES) / LANES
    c2, s2 = np.cos(ang2), np.sin(ang2)
    lane_fwd = np.block([[c2, -s2], [s2, c2]])
    lane_inv = np.block([[c2, s2], [-s2, c2]])
    leave = np.block([[c1.T, -s1.T], [s1.T, c1.T]]) / total
    leave_real = leave[:half] * scale
    phase = (np.arange(K1)[:, None] * np.arange(LANES)[None, :]) % total
    angt = 2.0 * np.pi * phase / total
    turn = np.concatenate([np.cos(angt), np.sin(angt)], 1).astype(np.float32)

    def left(table):
        high, low = split_np(table)
        return np.concatenate([high, high, low], 1)

    def right(table):
        high, low = split_np(table)
        return np.concatenate([high, high, low], 0)

    return (
        left(enter), left(enter_real), right(lane_fwd), right(lane_inv),
        left(leave), left(leave_real), turn,
    )


def parts(value, axis):
    high = value.astype(BF16)
    low = (value - high.astype(F32)).astype(BF16)
    return jnp.concatenate([high, low, high], axis)


def mm(a, b):
    return jnp.dot(a, b, preferred_element_type=F32)


def twist_forward(part, turn_cos, turn_sin):
    half = part.shape[0] // 2
    re, im = part[:half], part[half:]
    return jnp.concatenate(
        [re * turn_cos + im * turn_sin, im * turn_cos - re * turn_sin], 1
    )


def twist_back(part, turn_cos, turn_sin):
    re, im = part[:, :LANES], part[:, LANES:]
    return jnp.concatenate(
        [re * turn_cos - im * turn_sin, im * turn_cos + re * turn_sin], 0
    )


def pre_kernel(
    rows, own, core_ref, q_hbm, k_hbm, v_hbm, g_hbm, f_hbm, send_ref, q, k, v, g, f, hold, sems
):
    batch, chans = q.shape[0], q.shape[1]
    peers = chans // own
    copies = []
    for b in range(batch):
        for i, (src, dst) in enumerate(((k_hbm, k), (v_hbm, v), (g_hbm, g), (q_hbm, q))):
            copies.append(pltpu.make_async_copy(src.at[b], dst.at[b], sems.at[4 * b + i]))
    taps = pltpu.make_async_copy(f_hbm, f, sems.at[4 * batch])
    for copy in copies:
        copy.start()
    taps.start()
    for b in range(batch):
        for sig, (left, right) in enumerate(((k, v), (g, q))):
            copies[4 * b + 2 * sig].wait()
            copies[4 * b + 2 * sig + 1].wait()
            slot = hold.at[2 * b + sig]
            slot[...] = left[b].astype(F32) * right[b].astype(F32)
            for j in range(own):
                send_ref[pl.ds((sig * batch + b) * own + j, peers, stride=rows), :] = slot[
                    pl.ds(j, peers, stride=own), :
                ]
    taps.wait()
    send_ref[pl.ds(2 * batch * own, peers, stride=rows), :] = f[
        pl.ds(core_ref[0], peers, stride=own), :
    ]


def leave_product(table, data):
    depth = data.shape[0]
    high = data.astype(BF16)
    low = (data - high.astype(F32)).astype(BF16)
    first = table[:, :depth]
    return mm(first, high) + mm(first, low) + mm(table[:, 2 * depth :], high)


def mid_kernel(
    devices, groups, own, batch, rows_in, rows_out, r_ref, enter, enter_real, lane_fwd, lane_inv,
    leave, leave_real, turn_ref, send_ref,
):
    turn_cos, turn_sin = turn_ref[:, :LANES], turn_ref[:, LANES:]
    K1 = 2 * devices
    step_in, step_out = groups * rows_in, groups * rows_out

    def lanes(value, i):
        return value[:, i * LANES : (i + 1) * LANES]

    pieces = []
    for j in range(own):
        for sig in range(2):
            for d in range(groups):
                base = d * rows_in + sig * batch * own + j
                re = r_ref[pl.ds(base, devices, stride=step_in), :]
                im = r_ref[pl.ds(base + own, devices, stride=step_in), :]
                pieces.append(jnp.concatenate([re, im], 0))
    taps = [
        r_ref[pl.ds(j * rows_in + 2 * batch * own, devices, stride=step_in), :]
        for j in range(own)
    ]
    count = len(pieces)
    real = mm(enter_real[...], parts(jnp.concatenate(taps, 1), 0))
    full = mm(enter[...], parts(jnp.concatenate(pieces, 1), 0))
    turned = [twist_forward(lanes(real, j), turn_cos, turn_sin) for j in range(own)]
    turned += [twist_forward(lanes(full, i), turn_cos, turn_sin) for i in range(count)]
    spec = mm(parts(jnp.concatenate(turned, 0), 1), lane_fwd[...])

    def pair(i):
        rows = spec[i * K1 : (i + 1) * K1]
        return rows[:, :LANES], rows[:, LANES:]

    products, crosses = [], []
    for j in range(own):
        hr, hi = pair(j)
        cross_re = cross_im = 0.0
        conv, back = [], []
        for d in range(groups):
            mr, mi = pair(own + 2 * j * groups + d)
            wr, wi = pair(own + (2 * j + 1) * groups + d)
            conv.append(jnp.concatenate([mr * hr - mi * hi, mr * hi + mi * hr], 1))
            back.append(jnp.concatenate([wr * hr + wi * hi, wi * hr - wr * hi], 1))
            cross_re = cross_re + (wr * mr + wi * mi)
            cross_im = cross_im + (wi * mr - wr * mi)
        products += conv + back
        crosses.append(jnp.concatenate([cross_re, cross_im], 1))
    spread = mm(parts(jnp.concatenate(products + crosses, 0), 1), lane_inv[...])
    turned = [
        twist_back(spread[i * K1 : (i + 1) * K1], turn_cos, turn_sin)
        for i in range(count + own)
    ]
    final = leave_product(leave[...], jnp.concatenate(turned[:count], 1))
    terms = leave_product(leave_real[...], jnp.concatenate(turned[count:], 1))
    for j in range(own):
        for sig in range(2):
            for d in range(groups):
                part = lanes(final, (2 * j + sig) * groups + d)
                for b in range(batch):
                    base = d * rows_out + (sig * batch + b) * own + j
                    send_ref[pl.ds(base, devices, stride=step_out), :] = part[
                        b * devices : (b + 1) * devices
                    ]
        for d in range(j, groups, own):
            base = d * rows_out + 2 * batch * own
            send_ref[pl.ds(base, devices, stride=step_out), :] = lanes(terms, j)


def post_kernel(
    rows, own, r_ref, skip_ref, q_ref, k_ref, v_ref, g_ref, out_ref, gq_ref, gk_ref, gv_ref,
    conv_ref, back_ref,
):
    batch, chans = q_ref.shape[0], q_ref.shape[1]
    peers = chans // own
    skip = skip_ref[...]
    for b in range(batch):
        for j in range(own):
            conv_ref[pl.ds(j, peers, stride=own), :] = r_ref[
                pl.ds(b * own + j, peers, stride=rows), :
            ]
            back_ref[pl.ds(j, peers, stride=own), :] = r_ref[
                pl.ds((batch + b) * own + j, peers, stride=rows), :
            ]
        query, keys = q_ref[b].astype(F32), k_ref[b].astype(F32)
        values, upstream = v_ref[b].astype(F32), g_ref[b].astype(F32)
        gated = conv_ref[...] + skip * (keys * values)
        back = back_ref[...] + skip * (upstream * query)
        out_ref[b] = (query * gated).astype(BF16)
        gq_ref[b] = (upstream * gated).astype(BF16)
        gk_ref[b] = (back * values).astype(BF16)
        gv_ref[b] = (back * keys).astype(BF16)


def join_kernel(own, core_ref, mine_ref, other_ref, out_ref):
    peers = mine_ref.shape[0]
    core = core_ref[0]
    out_ref[pl.ds(core, peers, stride=own), :] = mine_ref[...]
    out_ref[pl.ds(own - 1 - core, peers, stride=own), :] = other_ref[...]


VMEM = pl.BlockSpec(memory_space=pltpu.VMEM)
SMEM = pl.BlockSpec(memory_space=pltpu.SMEM)
HBM = pl.BlockSpec(memory_space=pltpu.HBM)
MIB = 1024 * 1024


def shards(devices, groups, tables, query_proj, key_proj, value_proj, long_filter, skip_gain, out_grad):
    batch, chans, cols = query_proj.shape
    peers = devices * groups
    own = chans // peers
    rows_in = 2 * batch * own + 1
    rows_out = rows_in
    core = lax.rem(lax.axis_index("dp"), own).astype(jnp.int32).reshape(1)

    def params(mib):
        return pltpu.CompilerParams(vmem_limit_bytes=mib * MIB)

    def exchange(flat, rows):
        shaped = flat.reshape(peers, rows, 1, cols)
        moved = lax.all_to_all(shaped, ("seq", "dp"), split_axis=0, concat_axis=0, tiled=True)
        return moved.reshape(peers * rows, cols)

    with jax.named_scope("pre"):
        wide = pltpu.VMEM((batch, chans, cols), BF16)
        send = pl.pallas_call(
            lambda *refs: pre_kernel(rows_in, own, *refs),
            out_shape=jax.ShapeDtypeStruct((peers * rows_in, cols), F32),
            in_specs=[SMEM] + [HBM] * 5,
            out_specs=VMEM,
            scratch_shapes=[
                wide, wide, wide, wide,
                pltpu.VMEM((chans, cols), F32),
                pltpu.VMEM((2 * batch, chans, cols), F32),
                pltpu.SemaphoreType.DMA((4 * batch + 1,)),
            ],
            compiler_params=params(62),
        )(core, query_proj, key_proj, value_proj, out_grad, long_filter)
    with jax.named_scope("gather"):
        arrived = exchange(send, rows_in)
    with jax.named_scope("mid"):
        send = pl.pallas_call(
            lambda *refs: mid_kernel(devices, groups, own, batch, rows_in, rows_out, *refs),
            out_shape=jax.ShapeDtypeStruct((peers * rows_out, cols), F32),
            in_specs=[VMEM] * (1 + len(tables)),
            out_specs=VMEM,
            compiler_params=params(48),
        )(arrived, *tables)
    with jax.named_scope("scatter"):
        shaped = send.reshape(peers, rows_out, 1, cols)
        returned = lax.all_to_all(shaped, ("seq", "dp"), split_axis=0, concat_axis=0, tiled=True)
    with jax.named_scope("swap"):
        mine = returned[:, rows_out - 1].reshape(peers, cols)
        pairs = [(d, d + 1 - 2 * (d % own)) for d in range(groups)]
        other = lax.ppermute(mine, "dp", pairs)
    with jax.named_scope("post"):
        plane = jax.ShapeDtypeStruct((batch, chans, cols), BF16)
        planes = pl.pallas_call(
            lambda *refs: post_kernel(rows_out, own, *refs),
            out_shape=[plane] * 4,
            in_specs=[VMEM] * 6,
            out_specs=[VMEM] * 4,
            scratch_shapes=[pltpu.VMEM((chans, cols), F32)] * 2,
            compiler_params=params(48),
            cost_estimate=pl.CostEstimate(flops=10**6, bytes_accessed=4 * 10**6, transcendentals=0),
        )(returned.reshape(peers * rows_out, cols), skip_gain[:, None], query_proj, key_proj, value_proj, out_grad)
    with jax.named_scope("join"):
        grad_filter = pl.pallas_call(
            lambda *refs: join_kernel(own, *refs),
            out_shape=jax.ShapeDtypeStruct((chans, cols), F32),
            in_specs=[SMEM, VMEM, VMEM],
            out_specs=VMEM,
            compiler_params=params(48),
            cost_estimate=pl.CostEstimate(flops=10**5, bytes_accessed=5 * 10**5, transcendentals=0),
        )(core, mine, other)
    return (*planes, grad_filter)


def solution(mesh):
    devices, groups = mesh.shape["seq"], mesh.shape["dp"]
    tables = build_tables(devices, 1.0 / math.sqrt(2 * groups * devices * LANES))

    def run(*args):
        return shards(devices, groups, tables, *args)

    wide = P("dp", None, "seq")
    return jax.shard_map(
        run,
        mesh=mesh,
        in_specs=(wide, wide, wide, P(None, "seq"), P(), wide),
        out_specs=(wide, wide, wide, wide, P(None, "seq")),
        check_vma=False,
    )
```

```python
import math

import jax
import jax.numpy as jnp
import numpy as np
from jax import lax
from jax.experimental import pallas as pl
from jax.experimental.pallas import tpu as pltpu
from jax.sharding import PartitionSpec as P

F32 = jnp.float32
BF16 = jnp.bfloat16
LANES = 128
CHUNKS = 4


def split_np(table):
    high = table.astype(jnp.bfloat16)
    low = (table - high.astype(np.float64)).astype(jnp.bfloat16)
    return high, low


def build_tables(half, scale):
    K1 = 2 * half
    total = K1 * LANES
    k1 = np.arange(K1)[:, None]
    n1 = np.arange(half)[None, :]
    ang = 2.0 * np.pi * ((k1 * n1) % K1) / K1
    c1, s1 = np.cos(ang), np.sin(ang)
    enter = np.block([[c1, s1], [-s1, c1]])
    enter_real = np.concatenate([c1, -s1], 0)
    n2 = np.arange(LANES)[:, None]
    k2 = np.arange(LANES)[None, :]
    ang2 = 2.0 * np.pi * ((n2 * k2) % LANES) / LANES
    c2, s2 = np.cos(ang2), np.sin(ang2)
    lane_fwd = np.block([[c2, -s2], [s2, c2]])
    lane_inv = np.block([[c2, s2], [-s2, c2]])
    leave = np.block([[c1.T, -s1.T], [s1.T, c1.T]]) / total
    leave_real = leave[:half] * scale
    phase = (np.arange(K1)[:, None] * np.arange(LANES)[None, :]) % total
    angt = 2.0 * np.pi * phase / total
    turn = np.concatenate([np.cos(angt), np.sin(angt)], 1).astype(np.float32)

    def left(table):
        high, low = split_np(table)
        return np.concatenate([high, high, low], 1)

    def right(table):
        high, low = split_np(table)
        return np.concatenate([high, high, low], 0)

    return (
        left(enter), left(enter_real), right(lane_fwd), right(lane_inv),
        left(leave), left(leave_real), turn,
    )


def parts(value, axis):
    high = value.astype(BF16)
    low = (value - high.astype(F32)).astype(BF16)
    return jnp.concatenate([high, low, high], axis)


def mm(a, b):
    return jnp.dot(a, b, preferred_element_type=F32)


def twist_forward(part, turn_cos, turn_sin):
    half = part.shape[0] // 2
    re, im = part[:half], part[half:]
    return jnp.concatenate(
        [re * turn_cos + im * turn_sin, im * turn_cos - re * turn_sin], 1
    )


def twist_back(part, turn_cos, turn_sin):
    re, im = part[:, :LANES], part[:, LANES:]
    return jnp.concatenate(
        [re * turn_cos - im * turn_sin, im * turn_cos + re * turn_sin], 0
    )


def pre_kernel(
    rows, own, core_ref, q_hbm, k_hbm, v_hbm, g_hbm, f_hbm, send_hbm, q, k, v, g, f, send, hold,
    sems, out_sems,
):
    batch, chans = q.shape[0], q.shape[1]
    span = chans // CHUNKS
    peers = span // own
    copies = []
    for n in range(CHUNKS):
        part = pl.ds(n * span, span)
        for i, (src, dst) in enumerate(((k_hbm, k), (v_hbm, v), (g_hbm, g), (q_hbm, q))):
            copies.append(
                pltpu.make_async_copy(src.at[:, part], dst.at[:, part], sems.at[5 * n + i])
            )
        copies.append(pltpu.make_async_copy(f_hbm.at[part], f.at[part], sems.at[5 * n + 4]))
    for copy in copies:
        copy.start()
    sent = []
    for n in range(CHUNKS):
        part = pl.ds(n * span, span)
        base = n * peers * rows
        for sig, (left, right) in enumerate(((k, v), (g, q))):
            copies[5 * n + 2 * sig].wait()
            copies[5 * n + 2 * sig + 1].wait()
            for b in range(batch):
                slot = hold.at[(2 * n + sig) * batch + b]
                slot[...] = left[b, part].astype(F32) * right[b, part].astype(F32)
                for j in range(own):
                    at = base + (sig * batch + b) * own + j
                    send[pl.ds(at, peers, stride=rows), :] = slot[pl.ds(j, peers, stride=own), :]
        copies[5 * n + 4].wait()
        send[pl.ds(base + 2 * batch * own, peers, stride=rows), :] = f[
            pl.ds(n * span + core_ref[0], peers, stride=own), :
        ]
        block = pl.ds(base, peers * rows)
        sent.append(pltpu.make_async_copy(send.at[block], send_hbm.at[block], out_sems.at[n]))
        sent[n].start()
    for copy in sent:
        copy.wait()


def leave_product(table, data):
    depth = data.shape[0]
    high = data.astype(BF16)
    low = (data - high.astype(F32)).astype(BF16)
    first = table[:, :depth]
    return mm(first, high) + mm(first, low) + mm(table[:, 2 * depth :], high)


def mid_kernel(
    devices, groups, own, batch, rows_in, rows_out, r_ref, enter, enter_real, lane_fwd, lane_inv,
    leave, leave_real, turn_ref, send_ref,
):
    turn_cos, turn_sin = turn_ref[:, :LANES], turn_ref[:, LANES:]
    K1 = 2 * devices
    step_in, step_out = groups * rows_in, groups * rows_out

    def lanes(value, i):
        return value[:, i * LANES : (i + 1) * LANES]

    pieces = []
    for j in range(own):
        for sig in range(2):
            for d in range(groups):
                base = d * rows_in + sig * batch * own + j
                re = r_ref[pl.ds(base, devices, stride=step_in), :]
                im = r_ref[pl.ds(base + own, devices, stride=step_in), :]
                pieces.append(jnp.concatenate([re, im], 0))
    taps = [
        r_ref[pl.ds(j * rows_in + 2 * batch * own, devices, stride=step_in), :]
        for j in range(own)
    ]
    count = len(pieces)
    real = mm(enter_real[...], parts(jnp.concatenate(taps, 1), 0))
    full = mm(enter[...], parts(jnp.concatenate(pieces, 1), 0))
    turned = [twist_forward(lanes(real, j), turn_cos, turn_sin) for j in range(own)]
    turned += [twist_forward(lanes(full, i), turn_cos, turn_sin) for i in range(count)]
    spec = mm(parts(jnp.concatenate(turned, 0), 1), lane_fwd[...])

    def pair(i):
        rows = spec[i * K1 : (i + 1) * K1]
        return rows[:, :LANES], rows[:, LANES:]

    products, crosses = [], []
    for j in range(own):
        hr, hi = pair(j)
        cross_re = cross_im = 0.0
        conv, back = [], []
        for d in range(groups):
            mr, mi = pair(own + 2 * j * groups + d)
            wr, wi = pair(own + (2 * j + 1) * groups + d)
            conv.append(jnp.concatenate([mr * hr - mi * hi, mr * hi + mi * hr], 1))
            back.append(jnp.concatenate([wr * hr + wi * hi, wi * hr - wr * hi], 1))
            cross_re = cross_re + (wr * mr + wi * mi)
            cross_im = cross_im + (wi * mr - wr * mi)
        products += conv + back
        crosses.append(jnp.concatenate([cross_re, cross_im], 1))
    spread = mm(parts(jnp.concatenate(products + crosses, 0), 1), lane_inv[...])
    turned = [
        twist_back(spread[i * K1 : (i + 1) * K1], turn_cos, turn_sin)
        for i in range(count + own)
    ]
    final = leave_product(leave[...], jnp.concatenate(turned[:count], 1))
    terms = leave_product(leave_real[...], jnp.concatenate(turned[count:], 1))
    for j in range(own):
        for sig in range(2):
            for d in range(groups):
                part = lanes(final, (2 * j + sig) * groups + d)
                for b in range(batch):
                    base = d * rows_out + (sig * batch + b) * own + j
                    send_ref[pl.ds(base, devices, stride=step_out), :] = part[
                        b * devices : (b + 1) * devices
                    ]
        for d in range(j, groups, own):
            base = d * rows_out + 2 * batch * own
            send_ref[pl.ds(base, devices, stride=step_out), :] = lanes(terms, j)


def post_kernel(
    rows, own, r_ref, skip_ref, q_ref, k_ref, v_ref, g_ref, out_hbm, gq_hbm, gk_hbm, gv_hbm,
    out, gq, gk, gv, conv_ref, back_ref, sems,
):
    batch, chans = q_ref.shape[0], q_ref.shape[1]
    span = chans // CHUNKS
    peers = span // own
    sent = []
    for n in range(CHUNKS):
        part = pl.ds(n * span, span)
        skip = skip_ref[part, :]
        for b in range(batch):
            conv, back = conv_ref.at[n * batch + b], back_ref.at[n * batch + b]
            for j in range(own):
                at = n * peers * rows + b * own + j
                conv[pl.ds(j, peers, stride=own), :] = r_ref[pl.ds(at, peers, stride=rows), :]
                at += batch * own
                back[pl.ds(j, peers, stride=own), :] = r_ref[pl.ds(at, peers, stride=rows), :]
            query, keys = q_ref[b, part].astype(F32), k_ref[b, part].astype(F32)
            values, upstream = v_ref[b, part].astype(F32), g_ref[b, part].astype(F32)
            gated = conv[...] + skip * (keys * values)
            total = back[...] + skip * (upstream * query)
            out[b, part] = (query * gated).astype(BF16)
            gq[b, part] = (upstream * gated).astype(BF16)
            gk[b, part] = (total * values).astype(BF16)
            gv[b, part] = (total * keys).astype(BF16)
        for i, (src, dst) in enumerate(((out, out_hbm), (gq, gq_hbm), (gk, gk_hbm), (gv, gv_hbm))):
            copy = pltpu.make_async_copy(src.at[:, part], dst.at[:, part], sems.at[4 * n + i])
            copy.start()
            sent.append(copy)
    for copy in sent:
        copy.wait()


def join_kernel(own, core_ref, mine_ref, other_ref, out_ref):
    peers = mine_ref.shape[0]
    core = core_ref[0]
    out_ref[pl.ds(core, peers, stride=own), :] = mine_ref[...]
    out_ref[pl.ds(own - 1 - core, peers, stride=own), :] = other_ref[...]


VMEM = pl.BlockSpec(memory_space=pltpu.VMEM)
SMEM = pl.BlockSpec(memory_space=pltpu.SMEM)
HBM = pl.BlockSpec(memory_space=pltpu.HBM)
MIB = 1024 * 1024


def shards(devices, groups, tables, query_proj, key_proj, value_proj, long_filter, skip_gain, out_grad):
    batch, chans, cols = query_proj.shape
    peers = devices * groups
    own = chans // peers
    rows_in = 2 * batch * own + 1
    rows_out = rows_in
    core = lax.rem(lax.axis_index("dp"), own).astype(jnp.int32).reshape(1)

    def params(mib):
        return pltpu.CompilerParams(vmem_limit_bytes=mib * MIB)

    def exchange(flat, rows):
        shaped = flat.reshape(peers, rows, 1, cols)
        moved = lax.all_to_all(shaped, ("seq", "dp"), split_axis=0, concat_axis=0, tiled=True)
        return moved.reshape(peers * rows, cols)

    with jax.named_scope("pre"):
        wide = pltpu.VMEM((batch, chans, cols), BF16)
        send = pl.pallas_call(
            lambda *refs: pre_kernel(rows_in, own, *refs),
            out_shape=jax.ShapeDtypeStruct((peers * rows_in, cols), F32),
            in_specs=[SMEM] + [HBM] * 5,
            out_specs=HBM,
            scratch_shapes=[
                wide, wide, wide, wide,
                pltpu.VMEM((chans, cols), F32),
                pltpu.VMEM((peers * rows_in, cols), F32),
                pltpu.VMEM((2 * batch * CHUNKS, chans // CHUNKS, cols), F32),
                pltpu.SemaphoreType.DMA((5 * CHUNKS,)),
                pltpu.SemaphoreType.DMA((CHUNKS,)),
            ],
            compiler_params=params(62),
        )(core, query_proj, key_proj, value_proj, out_grad, long_filter)
    with jax.named_scope("gather"):
        arrived = exchange(send, rows_in)
    with jax.named_scope("mid"):
        send = pl.pallas_call(
            lambda *refs: mid_kernel(devices, groups, own, batch, rows_in, rows_out, *refs),
            out_shape=jax.ShapeDtypeStruct((peers * rows_out, cols), F32),
            in_specs=[VMEM] * (1 + len(tables)),
            out_specs=VMEM,
            compiler_params=params(48),
        )(arrived, *tables)
    with jax.named_scope("scatter"):
        shaped = send.reshape(peers, rows_out, 1, cols)
        returned = lax.all_to_all(shaped, ("seq", "dp"), split_axis=0, concat_axis=0, tiled=True)
    with jax.named_scope("swap"):
        mine = returned[:, rows_out - 1].reshape(peers, cols)
        pairs = [(d, d + 1 - 2 * (d % own)) for d in range(groups)]
        other = lax.ppermute(mine, "dp", pairs)
    with jax.named_scope("post"):
        plane = jax.ShapeDtypeStruct((batch, chans, cols), BF16)
        planes = pl.pallas_call(
            lambda *refs: post_kernel(rows_out, own, *refs),
            out_shape=[plane] * 4,
            in_specs=[VMEM] * 6,
            out_specs=[HBM] * 4,
            scratch_shapes=[wide] * 4
            + [pltpu.VMEM((batch * CHUNKS, chans // CHUNKS, cols), F32)] * 2
            + [pltpu.SemaphoreType.DMA((4 * CHUNKS,))],
            compiler_params=params(48),
            cost_estimate=pl.CostEstimate(flops=10**6, bytes_accessed=4 * 10**6, transcendentals=0),
        )(returned.reshape(peers * rows_out, cols), skip_gain[:, None], query_proj, key_proj, value_proj, out_grad)
    with jax.named_scope("join"):
        grad_filter = pl.pallas_call(
            lambda *refs: join_kernel(own, *refs),
            out_shape=jax.ShapeDtypeStruct((chans, cols), F32),
            in_specs=[SMEM, VMEM, VMEM],
            out_specs=VMEM,
            compiler_params=params(48),
            cost_estimate=pl.CostEstimate(flops=10**5, bytes_accessed=5 * 10**5, transcendentals=0),
        )(core, mine, other)
    return (*planes, grad_filter)


def solution(mesh):
    devices, groups = mesh.shape["seq"], mesh.shape["dp"]
    tables = build_tables(devices, 1.0 / math.sqrt(2 * groups * devices * LANES))

    def run(*args):
        return shards(devices, groups, tables, *args)

    wide = P("dp", None, "seq")
    return jax.shard_map(
        run,
        mesh=mesh,
        in_specs=(wide, wide, wide, P(None, "seq"), P(), wide),
        out_specs=(wide, wide, wide, wide, P(None, "seq")),
        check_vma=False,
    )
```

```python
import math

import jax
import jax.numpy as jnp
import numpy as np
from jax import lax
from jax.experimental import pallas as pl
from jax.experimental.pallas import tpu as pltpu
from jax.sharding import PartitionSpec as P

F32 = jnp.float32
BF16 = jnp.bfloat16
LANES = 128
CHUNKS = 4


def split_np(table):
    high = table.astype(jnp.bfloat16)
    low = (table - high.astype(np.float64)).astype(jnp.bfloat16)
    return high, low


def build_tables(half, scale):
    K1 = 2 * half
    total = K1 * LANES
    k1 = np.arange(K1)[:, None]
    n1 = np.arange(half)[None, :]
    ang = 2.0 * np.pi * ((k1 * n1) % K1) / K1
    c1, s1 = np.cos(ang), np.sin(ang)
    enter = np.block([[c1, s1], [-s1, c1]])
    enter_real = np.concatenate([c1, -s1], 0)
    n2 = np.arange(LANES)[:, None]
    k2 = np.arange(LANES)[None, :]
    ang2 = 2.0 * np.pi * ((n2 * k2) % LANES) / LANES
    c2, s2 = np.cos(ang2), np.sin(ang2)
    lane_fwd = np.block([[c2, -s2], [s2, c2]])
    lane_inv = np.block([[c2, s2], [-s2, c2]])
    leave = np.block([[c1.T, -s1.T], [s1.T, c1.T]]) / total
    leave_real = leave[:half] * scale
    phase = (np.arange(K1)[:, None] * np.arange(LANES)[None, :]) % total
    angt = 2.0 * np.pi * phase / total
    turn = np.concatenate([np.cos(angt), np.sin(angt)], 1).astype(np.float32)

    def left(table):
        high, low = split_np(table)
        return np.concatenate([high, high, low], 1)

    def right(table):
        high, low = split_np(table)
        return np.concatenate([high, high, low], 0)

    return (
        left(enter), left(enter_real), right(lane_fwd), right(lane_inv),
        left(leave), left(leave_real), turn,
    )


def parts(value, axis):
    high = value.astype(BF16)
    low = (value - high.astype(F32)).astype(BF16)
    return jnp.concatenate([high, low, high], axis)


def mm(a, b):
    return jnp.dot(a, b, preferred_element_type=F32)


def twist_forward(part, turn_cos, turn_sin):
    half = part.shape[0] // 2
    re, im = part[:half], part[half:]
    return jnp.concatenate(
        [re * turn_cos + im * turn_sin, im * turn_cos - re * turn_sin], 1
    )


def twist_back(part, turn_cos, turn_sin):
    re, im = part[:, :LANES], part[:, LANES:]
    return jnp.concatenate(
        [re * turn_cos - im * turn_sin, im * turn_cos + re * turn_sin], 0
    )


def pre_kernel(
    rows, own, core_ref, q_hbm, k_hbm, v_hbm, g_hbm, f_hbm, send_hbm, q, k, v, g, f, send, hold,
    sems, out_sems,
):
    batch, chans = q.shape[0], q.shape[1]
    span = chans // CHUNKS
    peers = span // own
    copies = []
    for n in range(CHUNKS):
        part = pl.ds(n * span, span)
        for i, (src, dst) in enumerate(((k_hbm, k), (v_hbm, v), (g_hbm, g), (q_hbm, q))):
            copies.append(
                pltpu.make_async_copy(src.at[:, part], dst.at[:, part], sems.at[5 * n + i])
            )
        copies.append(pltpu.make_async_copy(f_hbm.at[part], f.at[part], sems.at[5 * n + 4]))
    for copy in copies:
        copy.start()
    sent = []
    for n in range(CHUNKS):
        part = pl.ds(n * span, span)
        base = n * peers * rows
        for sig, (left, right) in enumerate(((k, v), (g, q))):
            copies[5 * n + 2 * sig].wait()
            copies[5 * n + 2 * sig + 1].wait()
            for b in range(batch):
                slot = hold.at[(2 * n + sig) * batch + b]
                slot[...] = left[b, part].astype(F32) * right[b, part].astype(F32)
                for j in range(own):
                    at = base + (sig * batch + b) * own + j
                    send[pl.ds(at, peers, stride=rows), :] = slot[pl.ds(j, peers, stride=own), :]
        copies[5 * n + 4].wait()
        send[pl.ds(base + 2 * batch * own, peers, stride=rows), :] = f[
            pl.ds(n * span + core_ref[0], peers, stride=own), :
        ]
        block = pl.ds(base, peers * rows)
        sent.append(pltpu.make_async_copy(send.at[block], send_hbm.at[block], out_sems.at[n]))
        sent[n].start()
    for copy in sent:
        copy.wait()


def leave_product(table, data):
    depth = data.shape[0]
    high = data.astype(BF16)
    low = (data - high.astype(F32)).astype(BF16)
    first = table[:, :depth]
    return mm(first, high) + mm(first, low) + mm(table[:, 2 * depth :], high)


def mid_kernel(
    devices, groups, own, batch, rows_in, rows_out, r_ref, enter, enter_real, lane_fwd, lane_inv,
    leave, leave_real, turn_ref, send_ref,
):
    turn_cos, turn_sin = turn_ref[:, :LANES], turn_ref[:, LANES:]
    K1 = 2 * devices
    step_in, step_out = groups * rows_in, groups * rows_out

    def lanes(value, i):
        return value[:, i * LANES : (i + 1) * LANES]

    def load(j, sig, d):
        base = d * rows_in + sig * batch * own + j
        re = r_ref[pl.ds(base, devices, stride=step_in), :]
        im = r_ref[pl.ds(base + own, devices, stride=step_in), :]
        return jnp.concatenate([re, im], 0)

    def forward(value, count):
        turned = [twist_forward(lanes(value, i), turn_cos, turn_sin) for i in range(count)]
        return mm(parts(jnp.concatenate(turned, 0), 1), lane_fwd[...])

    def inverse(spread, table, count):
        turned = [
            twist_back(spread[i * K1 : (i + 1) * K1], turn_cos, turn_sin) for i in range(count)
        ]
        return leave_product(table[...], jnp.concatenate(turned, 1))

    def pair(spec, i):
        rows = spec[i * K1 : (i + 1) * K1]
        return rows[:, :LANES], rows[:, LANES:]

    count = 2 * groups
    taps = [
        r_ref[pl.ds(j * rows_in + 2 * batch * own, devices, stride=step_in), :]
        for j in range(own)
    ]
    real = mm(enter_real[...], parts(jnp.concatenate(taps, 1), 0))
    taps_spec = forward(real, own)
    loaded = [
        jnp.concatenate([load(j, sig, d) for sig in range(2) for d in range(groups)], 1)
        for j in range(own)
    ]
    entered = [mm(enter[...], parts(value, 0)) for value in loaded]
    specs = [forward(value, count) for value in entered]
    spreads, crosses = [], []
    for j in range(own):
        hr, hi = pair(taps_spec, j)
        cross_re = cross_im = 0.0
        conv, back = [], []
        for d in range(groups):
            mr, mi = pair(specs[j], d)
            wr, wi = pair(specs[j], groups + d)
            conv.append(jnp.concatenate([mr * hr - mi * hi, mr * hi + mi * hr], 1))
            back.append(jnp.concatenate([wr * hr + wi * hi, wi * hr - wr * hi], 1))
            cross_re = cross_re + (wr * mr + wi * mi)
            cross_im = cross_im + (wi * mr - wr * mi)
        spreads.append(mm(parts(jnp.concatenate(conv + back, 0), 1), lane_inv[...]))
        crosses.append(jnp.concatenate([cross_re, cross_im], 1))
    cross_spread = mm(parts(jnp.concatenate(crosses, 0), 1), lane_inv[...])
    for j in range(own):
        final = inverse(spreads[j], leave, count)
        for sig in range(2):
            for d in range(groups):
                part = lanes(final, sig * groups + d)
                for b in range(batch):
                    base = d * rows_out + (sig * batch + b) * own + j
                    send_ref[pl.ds(base, devices, stride=step_out), :] = part[
                        b * devices : (b + 1) * devices
                    ]
    terms = inverse(cross_spread, leave_real, own)
    for j in range(own):
        for d in range(j, groups, own):
            base = d * rows_out + 2 * batch * own
            send_ref[pl.ds(base, devices, stride=step_out), :] = lanes(terms, j)


def post_kernel(
    rows, own, r_ref, skip_ref, q_ref, k_ref, v_ref, g_ref, out_hbm, gq_hbm, gk_hbm, gv_hbm,
    out, gq, gk, gv, conv_ref, back_ref, sems,
):
    batch, chans = q_ref.shape[0], q_ref.shape[1]
    span = chans // CHUNKS
    peers = span // own
    sent = []
    for n in range(CHUNKS):
        part = pl.ds(n * span, span)
        skip = skip_ref[part, :]
        for b in range(batch):
            conv, back = conv_ref.at[n * batch + b], back_ref.at[n * batch + b]
            for j in range(own):
                at = n * peers * rows + b * own + j
                conv[pl.ds(j, peers, stride=own), :] = r_ref[pl.ds(at, peers, stride=rows), :]
                at += batch * own
                back[pl.ds(j, peers, stride=own), :] = r_ref[pl.ds(at, peers, stride=rows), :]
            query, keys = q_ref[b, part].astype(F32), k_ref[b, part].astype(F32)
            values, upstream = v_ref[b, part].astype(F32), g_ref[b, part].astype(F32)
            gated = conv[...] + skip * (keys * values)
            total = back[...] + skip * (upstream * query)
            out[b, part] = (query * gated).astype(BF16)
            gq[b, part] = (upstream * gated).astype(BF16)
            gk[b, part] = (total * values).astype(BF16)
            gv[b, part] = (total * keys).astype(BF16)
        for i, (src, dst) in enumerate(((out, out_hbm), (gq, gq_hbm), (gk, gk_hbm), (gv, gv_hbm))):
            copy = pltpu.make_async_copy(src.at[:, part], dst.at[:, part], sems.at[4 * n + i])
            copy.start()
            sent.append(copy)
    for copy in sent:
        copy.wait()


def join_kernel(own, core_ref, mine_ref, other_ref, out_ref):
    peers = mine_ref.shape[0]
    core = core_ref[0]
    out_ref[pl.ds(core, peers, stride=own), :] = mine_ref[...]
    out_ref[pl.ds(own - 1 - core, peers, stride=own), :] = other_ref[...]


VMEM = pl.BlockSpec(memory_space=pltpu.VMEM)
SMEM = pl.BlockSpec(memory_space=pltpu.SMEM)
HBM = pl.BlockSpec(memory_space=pltpu.HBM)
MIB = 1024 * 1024


def shards(devices, groups, tables, query_proj, key_proj, value_proj, long_filter, skip_gain, out_grad):
    batch, chans, cols = query_proj.shape
    peers = devices * groups
    own = chans // peers
    rows_in = 2 * batch * own + 1
    rows_out = rows_in
    core = lax.rem(lax.axis_index("dp"), own).astype(jnp.int32).reshape(1)

    def params(mib):
        return pltpu.CompilerParams(vmem_limit_bytes=mib * MIB)

    def exchange(flat, rows):
        shaped = flat.reshape(peers, rows, 1, cols)
        moved = lax.all_to_all(shaped, ("seq", "dp"), split_axis=0, concat_axis=0, tiled=True)
        return moved.reshape(peers * rows, cols)

    with jax.named_scope("pre"):
        wide = pltpu.VMEM((batch, chans, cols), BF16)
        send = pl.pallas_call(
            lambda *refs: pre_kernel(rows_in, own, *refs),
            out_shape=jax.ShapeDtypeStruct((peers * rows_in, cols), F32),
            in_specs=[SMEM] + [HBM] * 5,
            out_specs=HBM,
            scratch_shapes=[
                wide, wide, wide, wide,
                pltpu.VMEM((chans, cols), F32),
                pltpu.VMEM((peers * rows_in, cols), F32),
                pltpu.VMEM((2 * batch * CHUNKS, chans // CHUNKS, cols), F32),
                pltpu.SemaphoreType.DMA((5 * CHUNKS,)),
                pltpu.SemaphoreType.DMA((CHUNKS,)),
            ],
            compiler_params=params(62),
        )(core, query_proj, key_proj, value_proj, out_grad, long_filter)
    with jax.named_scope("gather"):
        arrived = exchange(send, rows_in)
    with jax.named_scope("mid"):
        send = pl.pallas_call(
            lambda *refs: mid_kernel(devices, groups, own, batch, rows_in, rows_out, *refs),
            out_shape=jax.ShapeDtypeStruct((peers * rows_out, cols), F32),
            in_specs=[VMEM] * (1 + len(tables)),
            out_specs=VMEM,
            compiler_params=params(48),
        )(arrived, *tables)
    with jax.named_scope("scatter"):
        shaped = send.reshape(peers, rows_out, 1, cols)
        returned = lax.all_to_all(shaped, ("seq", "dp"), split_axis=0, concat_axis=0, tiled=True)
    with jax.named_scope("swap"):
        mine = returned[:, rows_out - 1].reshape(peers, cols)
        pairs = [(d, d + 1 - 2 * (d % own)) for d in range(groups)]
        other = lax.ppermute(mine, "dp", pairs)
    with jax.named_scope("post"):
        plane = jax.ShapeDtypeStruct((batch, chans, cols), BF16)
        planes = pl.pallas_call(
            lambda *refs: post_kernel(rows_out, own, *refs),
            out_shape=[plane] * 4,
            in_specs=[VMEM] * 6,
            out_specs=[HBM] * 4,
            scratch_shapes=[wide] * 4
            + [pltpu.VMEM((batch * CHUNKS, chans // CHUNKS, cols), F32)] * 2
            + [pltpu.SemaphoreType.DMA((4 * CHUNKS,))],
            compiler_params=params(48),
            cost_estimate=pl.CostEstimate(flops=10**6, bytes_accessed=4 * 10**6, transcendentals=0),
        )(returned.reshape(peers * rows_out, cols), skip_gain[:, None], query_proj, key_proj, value_proj, out_grad)
    with jax.named_scope("join"):
        grad_filter = pl.pallas_call(
            lambda *refs: join_kernel(own, *refs),
            out_shape=jax.ShapeDtypeStruct((chans, cols), F32),
            in_specs=[SMEM, VMEM, VMEM],
            out_specs=VMEM,
            compiler_params=params(48),
            cost_estimate=pl.CostEstimate(flops=10**5, bytes_accessed=5 * 10**5, transcendentals=0),
        )(core, mine, other)
    return (*planes, grad_filter)


def solution(mesh):
    devices, groups = mesh.shape["seq"], mesh.shape["dp"]
    tables = build_tables(devices, 1.0 / math.sqrt(2 * groups * devices * LANES))

    def run(*args):
        return shards(devices, groups, tables, *args)

    wide = P("dp", None, "seq")
    return jax.shard_map(
        run,
        mesh=mesh,
        in_specs=(wide, wide, wide, P(None, "seq"), P(), wide),
        out_specs=(wide, wide, wide, wide, P(None, "seq")),
        check_vma=False,
    )
```

```python
import math

import jax
import jax.numpy as jnp
import numpy as np
from jax import lax
from jax.experimental import pallas as pl
from jax.experimental.pallas import tpu as pltpu
from jax.sharding import PartitionSpec as P

F32 = jnp.float32
BF16 = jnp.bfloat16
LANES = 128
CHUNKS = 4


def split_np(table):
    high = table.astype(jnp.bfloat16)
    low = (table - high.astype(np.float64)).astype(jnp.bfloat16)
    return high, low


def build_tables(half, scale):
    K1 = 2 * half
    total = K1 * LANES
    k1 = np.arange(K1)[:, None]
    n1 = np.arange(half)[None, :]
    ang = 2.0 * np.pi * ((k1 * n1) % K1) / K1
    c1, s1 = np.cos(ang), np.sin(ang)
    enter = np.block([[c1, s1], [-s1, c1]])
    enter_real = np.concatenate([c1, -s1], 0)
    n2 = np.arange(LANES)[:, None]
    k2 = np.arange(LANES)[None, :]
    ang2 = 2.0 * np.pi * ((n2 * k2) % LANES) / LANES
    c2, s2 = np.cos(ang2), np.sin(ang2)
    lane_fwd = np.block([[c2, -s2], [s2, c2]])
    lane_inv = np.block([[c2, s2], [-s2, c2]])
    leave = np.block([[c1.T, -s1.T], [s1.T, c1.T]]) / total
    leave_real = leave[:half] * scale
    phase = (np.arange(K1)[:, None] * np.arange(LANES)[None, :]) % total
    angt = 2.0 * np.pi * phase / total
    turn = np.concatenate([np.cos(angt), np.sin(angt)], 1).astype(np.float32)

    def left(table):
        high, low = split_np(table)
        return np.concatenate([high, high, low], 1)

    def right(table):
        high, low = split_np(table)
        return np.concatenate([high, high, low], 0)

    return (
        left(enter), left(enter_real), right(lane_fwd), right(lane_inv),
        left(leave), left(leave_real), turn,
    )


def parts(value, axis):
    high = value.astype(BF16)
    low = (value - high.astype(F32)).astype(BF16)
    return jnp.concatenate([high, low, high], axis)


def mm(a, b):
    return jnp.dot(a, b, preferred_element_type=F32)


def twist_forward(part, turn_cos, turn_sin):
    half = part.shape[0] // 2
    re, im = part[:half], part[half:]
    return jnp.concatenate(
        [re * turn_cos + im * turn_sin, im * turn_cos - re * turn_sin], 1
    )


def twist_back(part, turn_cos, turn_sin):
    re, im = part[:, :LANES], part[:, LANES:]
    return jnp.concatenate(
        [re * turn_cos - im * turn_sin, im * turn_cos + re * turn_sin], 0
    )


def pre_kernel(
    rows, own, core_ref, q_hbm, k_hbm, v_hbm, g_hbm, f_hbm, send_hbm, q, k, v, g, f, send, hold,
    sems, out_sems,
):
    batch, chans = q.shape[0], q.shape[1]
    span = chans // CHUNKS
    peers = span // own
    copies = []
    for n in range(CHUNKS):
        part = pl.ds(n * span, span)
        for i, (src, dst) in enumerate(((k_hbm, k), (v_hbm, v), (g_hbm, g), (q_hbm, q))):
            copies.append(
                pltpu.make_async_copy(src.at[:, part], dst.at[:, part], sems.at[5 * n + i])
            )
        copies.append(pltpu.make_async_copy(f_hbm.at[part], f.at[part], sems.at[5 * n + 4]))
    for copy in copies:
        copy.start()
    sent = []
    for n in range(CHUNKS):
        part = pl.ds(n * span, span)
        base = n * peers * rows
        for sig, (left, right) in enumerate(((k, v), (g, q))):
            copies[5 * n + 2 * sig].wait()
            copies[5 * n + 2 * sig + 1].wait()
            for b in range(batch):
                slot = hold.at[(2 * n + sig) * batch + b]
                slot[...] = left[b, part].astype(F32) * right[b, part].astype(F32)
                for j in range(own):
                    at = base + (sig * batch + b) * own + j
                    send[pl.ds(at, peers, stride=rows), :] = slot[pl.ds(j, peers, stride=own), :]
        copies[5 * n + 4].wait()
        row = f[pl.ds(n * span, peers, stride=own), :]
        for j in range(1, own):
            row = jnp.where(core_ref[0] == j, f[pl.ds(n * span + j, peers, stride=own), :], row)
        send[pl.ds(base + 2 * batch * own, peers, stride=rows), :] = row
        block = pl.ds(base, peers * rows)
        sent.append(pltpu.make_async_copy(send.at[block], send_hbm.at[block], out_sems.at[n]))
        sent[n].start()
    for copy in sent:
        copy.wait()


def leave_product(table, data):
    depth = data.shape[0]
    high = data.astype(BF16)
    low = (data - high.astype(F32)).astype(BF16)
    first = table[:, :depth]
    return mm(first, high) + mm(first, low) + mm(table[:, 2 * depth :], high)


def mid_kernel(
    devices, groups, own, batch, rows_in, rows_out, r_ref, enter, enter_real, lane_fwd, lane_inv,
    leave, leave_real, turn_ref, send_ref,
):
    turn_cos, turn_sin = turn_ref[:, :LANES], turn_ref[:, LANES:]
    K1 = 2 * devices
    step_in, step_out = groups * rows_in, groups * rows_out

    def lanes(value, i):
        return value[:, i * LANES : (i + 1) * LANES]

    def load(j, sig, d):
        base = d * rows_in + sig * batch * own + j
        re = r_ref[pl.ds(base, devices, stride=step_in), :]
        im = r_ref[pl.ds(base + own, devices, stride=step_in), :]
        return jnp.concatenate([re, im], 0)

    def forward(value, count):
        turned = [twist_forward(lanes(value, i), turn_cos, turn_sin) for i in range(count)]
        return mm(parts(jnp.concatenate(turned, 0), 1), lane_fwd[...])

    def inverse(spread, table, count):
        turned = [
            twist_back(spread[i * K1 : (i + 1) * K1], turn_cos, turn_sin) for i in range(count)
        ]
        return leave_product(table[...], jnp.concatenate(turned, 1))

    def pair(spec, i):
        rows = spec[i * K1 : (i + 1) * K1]
        return rows[:, :LANES], rows[:, LANES:]

    count = 2 * groups
    taps = [
        r_ref[pl.ds(j * rows_in + 2 * batch * own, devices, stride=step_in), :]
        for j in range(own)
    ]
    loaded = [
        jnp.concatenate([load(j, sig, d) for sig in range(2) for d in range(groups)], 1)
        for j in range(own)
    ]
    entered = [mm(enter[...], parts(value, 0)) for value in loaded]
    real = mm(enter_real[...], parts(jnp.concatenate(taps, 1), 0))
    taps_spec = forward(real, own)
    specs = [forward(value, count) for value in entered]
    spreads, crosses = [], []
    for j in range(own):
        hr, hi = pair(taps_spec, j)
        cross_re = cross_im = 0.0
        conv, back = [], []
        for d in range(groups):
            mr, mi = pair(specs[j], d)
            wr, wi = pair(specs[j], groups + d)
            conv.append(jnp.concatenate([mr * hr - mi * hi, mr * hi + mi * hr], 1))
            back.append(jnp.concatenate([wr * hr + wi * hi, wi * hr - wr * hi], 1))
            cross_re = cross_re + (wr * mr + wi * mi)
            cross_im = cross_im + (wi * mr - wr * mi)
        spreads.append(mm(parts(jnp.concatenate(conv + back, 0), 1), lane_inv[...]))
        crosses.append(jnp.concatenate([cross_re, cross_im], 1))
    cross_spread = mm(parts(jnp.concatenate(crosses, 0), 1), lane_inv[...])
    for j in range(own):
        final = inverse(spreads[j], leave, count)
        for sig in range(2):
            for d in range(groups):
                part = lanes(final, sig * groups + d)
                for b in range(batch):
                    base = d * rows_out + (sig * batch + b) * own + j
                    send_ref[pl.ds(base, devices, stride=step_out), :] = part[
                        b * devices : (b + 1) * devices
                    ]
    terms = inverse(cross_spread, leave_real, own)
    for j in range(own):
        for d in range(j, groups, own):
            base = d * rows_out + 2 * batch * own
            send_ref[pl.ds(base, devices, stride=step_out), :] = lanes(terms, j)


def post_kernel(
    rows, own, r_ref, skip_ref, q_ref, k_ref, v_ref, g_ref, out_hbm, gq_hbm, gk_hbm, gv_hbm,
    out, gq, gk, gv, conv_ref, back_ref, sems,
):
    batch, chans = q_ref.shape[0], q_ref.shape[1]
    span = chans // CHUNKS
    peers = span // own
    sent = []
    for n in range(CHUNKS):
        part = pl.ds(n * span, span)
        skip = skip_ref[part, :]
        for b in range(batch):
            conv, back = conv_ref.at[n * batch + b], back_ref.at[n * batch + b]
            for j in range(own):
                at = n * peers * rows + b * own + j
                conv[pl.ds(j, peers, stride=own), :] = r_ref[pl.ds(at, peers, stride=rows), :]
                at += batch * own
                back[pl.ds(j, peers, stride=own), :] = r_ref[pl.ds(at, peers, stride=rows), :]
            query, keys = q_ref[b, part].astype(F32), k_ref[b, part].astype(F32)
            values, upstream = v_ref[b, part].astype(F32), g_ref[b, part].astype(F32)
            gated = conv[...] + skip * (keys * values)
            total = back[...] + skip * (upstream * query)
            out[b, part] = (query * gated).astype(BF16)
            gq[b, part] = (upstream * gated).astype(BF16)
            gk[b, part] = (total * values).astype(BF16)
            gv[b, part] = (total * keys).astype(BF16)
        for i, (src, dst) in enumerate(((out, out_hbm), (gq, gq_hbm), (gk, gk_hbm), (gv, gv_hbm))):
            copy = pltpu.make_async_copy(src.at[:, part], dst.at[:, part], sems.at[4 * n + i])
            copy.start()
            sent.append(copy)
    for copy in sent:
        copy.wait()


def join_kernel(own, core_ref, mine_ref, other_ref, out_ref):
    peers = mine_ref.shape[0]
    for j in range(own):
        out_ref[pl.ds(j, peers, stride=own), :] = jnp.where(
            core_ref[0] == j, mine_ref[...], other_ref[...]
        )


VMEM = pl.BlockSpec(memory_space=pltpu.VMEM)
SMEM = pl.BlockSpec(memory_space=pltpu.SMEM)
HBM = pl.BlockSpec(memory_space=pltpu.HBM)
MIB = 1024 * 1024


def shards(devices, groups, tables, query_proj, key_proj, value_proj, long_filter, skip_gain, out_grad):
    batch, chans, cols = query_proj.shape
    peers = devices * groups
    own = chans // peers
    rows_in = 2 * batch * own + 1
    rows_out = rows_in
    core = lax.rem(lax.axis_index("dp"), own).astype(jnp.int32).reshape(1)

    def params(mib):
        return pltpu.CompilerParams(vmem_limit_bytes=mib * MIB)

    def exchange(flat, rows):
        shaped = flat.reshape(peers, rows, 1, cols)
        moved = lax.all_to_all(shaped, ("seq", "dp"), split_axis=0, concat_axis=0, tiled=True)
        return moved.reshape(peers * rows, cols)

    with jax.named_scope("pre"):
        wide = pltpu.VMEM((batch, chans, cols), BF16)
        send = pl.pallas_call(
            lambda *refs: pre_kernel(rows_in, own, *refs),
            out_shape=jax.ShapeDtypeStruct((peers * rows_in, cols), F32),
            in_specs=[SMEM] + [HBM] * 5,
            out_specs=HBM,
            scratch_shapes=[
                wide, wide, wide, wide,
                pltpu.VMEM((chans, cols), F32),
                pltpu.VMEM((peers * rows_in, cols), F32),
                pltpu.VMEM((2 * batch * CHUNKS, chans // CHUNKS, cols), F32),
                pltpu.SemaphoreType.DMA((5 * CHUNKS,)),
                pltpu.SemaphoreType.DMA((CHUNKS,)),
            ],
            compiler_params=params(62),
        )(core, query_proj, key_proj, value_proj, out_grad, long_filter)
    with jax.named_scope("gather"):
        arrived = exchange(send, rows_in)
    with jax.named_scope("mid"):
        send = pl.pallas_call(
            lambda *refs: mid_kernel(devices, groups, own, batch, rows_in, rows_out, *refs),
            out_shape=jax.ShapeDtypeStruct((peers * rows_out, cols), F32),
            in_specs=[VMEM] * (1 + len(tables)),
            out_specs=VMEM,
            compiler_params=params(48),
        )(arrived, *tables)
    with jax.named_scope("scatter"):
        shaped = send.reshape(peers, rows_out, 1, cols)
        returned = lax.all_to_all(shaped, ("seq", "dp"), split_axis=0, concat_axis=0, tiled=True)
    with jax.named_scope("swap"):
        mine = returned[:, rows_out - 1].reshape(peers, cols)
        pairs = [(d, d + 1 - 2 * (d % own)) for d in range(groups)]
        other = lax.ppermute(mine, "dp", pairs)
    with jax.named_scope("post"):
        plane = jax.ShapeDtypeStruct((batch, chans, cols), BF16)
        planes = pl.pallas_call(
            lambda *refs: post_kernel(rows_out, own, *refs),
            out_shape=[plane] * 4,
            in_specs=[VMEM] * 6,
            out_specs=[HBM] * 4,
            scratch_shapes=[wide] * 4
            + [pltpu.VMEM((batch * CHUNKS, chans // CHUNKS, cols), F32)] * 2
            + [pltpu.SemaphoreType.DMA((4 * CHUNKS,))],
            compiler_params=params(48),
            cost_estimate=pl.CostEstimate(flops=10**6, bytes_accessed=4 * 10**6, transcendentals=0),
        )(returned.reshape(peers * rows_out, cols), skip_gain[:, None], query_proj, key_proj, value_proj, out_grad)
    with jax.named_scope("join"):
        grad_filter = pl.pallas_call(
            lambda *refs: join_kernel(own, *refs),
            out_shape=jax.ShapeDtypeStruct((chans, cols), F32),
            in_specs=[SMEM, VMEM, VMEM],
            out_specs=VMEM,
            compiler_params=params(48),
            cost_estimate=pl.CostEstimate(flops=10**5, bytes_accessed=5 * 10**5, transcendentals=0),
        )(core, mine, other)
    return (*planes, grad_filter)


def solution(mesh):
    devices, groups = mesh.shape["seq"], mesh.shape["dp"]
    tables = build_tables(devices, 1.0 / math.sqrt(2 * groups * devices * LANES))

    def run(*args):
        return shards(devices, groups, tables, *args)

    wide = P("dp", None, "seq")
    return jax.shard_map(
        run,
        mesh=mesh,
        in_specs=(wide, wide, wide, P(None, "seq"), P(), wide),
        out_specs=(wide, wide, wide, wide, P(None, "seq")),
        check_vma=False,
    )
```

```python
import math

import jax
import jax.numpy as jnp
import numpy as np
from jax import lax
from jax.experimental import pallas as pl
from jax.experimental.pallas import tpu as pltpu
from jax.sharding import PartitionSpec as P

F32 = jnp.float32
BF16 = jnp.bfloat16
LANES = 128
CHUNKS = 4


def split_np(table):
    high = table.astype(jnp.bfloat16)
    low = (table - high.astype(np.float64)).astype(jnp.bfloat16)
    return high, low


def build_tables(half, scale):
    K1 = 2 * half
    total = K1 * LANES
    k1 = np.arange(K1)[:, None]
    n1 = np.arange(half)[None, :]
    ang = 2.0 * np.pi * ((k1 * n1) % K1) / K1
    c1, s1 = np.cos(ang), np.sin(ang)
    enter = np.block([[c1, s1], [-s1, c1]])
    enter_real = np.concatenate([c1, -s1], 0)
    n2 = np.arange(LANES)[:, None]
    k2 = np.arange(LANES)[None, :]
    ang2 = 2.0 * np.pi * ((n2 * k2) % LANES) / LANES
    c2, s2 = np.cos(ang2), np.sin(ang2)
    lane_fwd = np.block([[c2, -s2], [s2, c2]])
    lane_inv = np.block([[c2, s2], [-s2, c2]])
    leave = np.block([[c1.T, -s1.T], [s1.T, c1.T]]) / total
    leave_real = leave[:half] * scale
    phase = (np.arange(K1)[:, None] * np.arange(LANES)[None, :]) % total
    angt = 2.0 * np.pi * phase / total
    turn = np.concatenate([np.cos(angt), np.sin(angt)], 1).astype(np.float32)

    def left(table):
        high, low = split_np(table)
        return np.concatenate([high, high, low], 1)

    def right(table):
        high, low = split_np(table)
        return np.concatenate([high, high, low], 0)

    return (
        left(enter), left(enter_real), right(lane_fwd), right(lane_inv),
        left(leave), left(leave_real), turn,
    )


def parts(value, axis):
    high = value.astype(BF16)
    low = (value - high.astype(F32)).astype(BF16)
    return jnp.concatenate([high, low, high], axis)


def mm(a, b):
    return jnp.dot(a, b, preferred_element_type=F32)


def twist_forward(part, turn_cos, turn_sin):
    half = part.shape[0] // 2
    re, im = part[:half], part[half:]
    return jnp.concatenate(
        [re * turn_cos + im * turn_sin, im * turn_cos - re * turn_sin], 1
    )


def twist_back(part, turn_cos, turn_sin):
    re, im = part[:, :LANES], part[:, LANES:]
    return jnp.concatenate(
        [re * turn_cos - im * turn_sin, im * turn_cos + re * turn_sin], 0
    )


def pre_kernel(
    rows, own, core_ref, q_hbm, k_hbm, v_hbm, g_hbm, f_hbm, send, q, k, v, g, f, hold, sems
):
    batch, chans = q.shape[0], q.shape[1]
    span = chans // CHUNKS
    peers = span // own
    copies = []
    for n in range(CHUNKS):
        part = pl.ds(n * span, span)
        for i, (src, dst) in enumerate(((k_hbm, k), (v_hbm, v), (g_hbm, g), (q_hbm, q))):
            copies.append(
                pltpu.make_async_copy(src.at[:, part], dst.at[:, part], sems.at[5 * n + i])
            )
        copies.append(pltpu.make_async_copy(f_hbm.at[part], f.at[part], sems.at[5 * n + 4]))
    for copy in copies:
        copy.start()
    for n in range(CHUNKS):
        part = pl.ds(n * span, span)
        base = n * peers * rows
        for sig, (left, right) in enumerate(((k, v), (g, q))):
            copies[5 * n + 2 * sig].wait()
            copies[5 * n + 2 * sig + 1].wait()
            for b in range(batch):
                slot = hold.at[(2 * n + sig) * batch + b]
                slot[...] = left[b, part].astype(F32) * right[b, part].astype(F32)
                for j in range(own):
                    at = base + (sig * batch + b) * own + j
                    send[pl.ds(at, peers, stride=rows), :] = slot[pl.ds(j, peers, stride=own), :]
        copies[5 * n + 4].wait()
        row = f[pl.ds(n * span, peers, stride=own), :]
        for j in range(1, own):
            row = jnp.where(core_ref[0] == j, f[pl.ds(n * span + j, peers, stride=own), :], row)
        send[pl.ds(base + 2 * batch * own, peers, stride=rows), :] = row


def leave_product(table, data):
    depth = data.shape[0]
    high = data.astype(BF16)
    low = (data - high.astype(F32)).astype(BF16)
    first = table[:, :depth]
    return mm(first, high) + mm(first, low) + mm(table[:, 2 * depth :], high)


def mid_kernel(
    devices, groups, own, batch, rows_in, rows_out, r_ref, enter, enter_real, lane_fwd, lane_inv,
    leave, leave_real, turn_ref, send_ref,
):
    turn_cos, turn_sin = turn_ref[:, :LANES], turn_ref[:, LANES:]
    K1 = 2 * devices
    step_in, step_out = groups * rows_in, groups * rows_out

    def lanes(value, i):
        return value[:, i * LANES : (i + 1) * LANES]

    def load(j, sig, d):
        base = d * rows_in + sig * batch * own + j
        re = r_ref[pl.ds(base, devices, stride=step_in), :]
        im = r_ref[pl.ds(base + own, devices, stride=step_in), :]
        return jnp.concatenate([re, im], 0)

    def forward(value, count):
        turned = [twist_forward(lanes(value, i), turn_cos, turn_sin) for i in range(count)]
        return mm(parts(jnp.concatenate(turned, 0), 1), lane_fwd[...])

    def inverse(spread, table, count):
        turned = [
            twist_back(spread[i * K1 : (i + 1) * K1], turn_cos, turn_sin) for i in range(count)
        ]
        return leave_product(table[...], jnp.concatenate(turned, 1))

    def pair(spec, i):
        rows = spec[i * K1 : (i + 1) * K1]
        return rows[:, :LANES], rows[:, LANES:]

    count = 2 * groups
    taps = [
        r_ref[pl.ds(j * rows_in + 2 * batch * own, devices, stride=step_in), :]
        for j in range(own)
    ]
    loaded = [
        jnp.concatenate([load(j, sig, d) for sig in range(2) for d in range(groups)], 1)
        for j in range(own)
    ]
    entered = [mm(enter[...], parts(value, 0)) for value in loaded]
    real = mm(enter_real[...], parts(jnp.concatenate(taps, 1), 0))
    taps_spec = forward(real, own)
    specs = [forward(value, count) for value in entered]
    spreads, crosses = [], []
    for j in range(own):
        hr, hi = pair(taps_spec, j)
        cross_re = cross_im = 0.0
        conv, back = [], []
        for d in range(groups):
            mr, mi = pair(specs[j], d)
            wr, wi = pair(specs[j], groups + d)
            conv.append(jnp.concatenate([mr * hr - mi * hi, mr * hi + mi * hr], 1))
            back.append(jnp.concatenate([wr * hr + wi * hi, wi * hr - wr * hi], 1))
            cross_re = cross_re + (wr * mr + wi * mi)
            cross_im = cross_im + (wi * mr - wr * mi)
        spreads.append(mm(parts(jnp.concatenate(conv + back, 0), 1), lane_inv[...]))
        crosses.append(jnp.concatenate([cross_re, cross_im], 1))
    cross_spread = mm(parts(jnp.concatenate(crosses, 0), 1), lane_inv[...])
    for j in range(own):
        final = inverse(spreads[j], leave, count)
        for sig in range(2):
            for d in range(groups):
                part = lanes(final, sig * groups + d)
                for b in range(batch):
                    base = d * rows_out + (sig * batch + b) * own + j
                    send_ref[pl.ds(base, devices, stride=step_out), :] = part[
                        b * devices : (b + 1) * devices
                    ]
    terms = inverse(cross_spread, leave_real, own)
    for j in range(own):
        for d in range(j, groups, own):
            base = d * rows_out + 2 * batch * own
            send_ref[pl.ds(base, devices, stride=step_out), :] = lanes(terms, j)


def post_kernel(
    rows, own, r_ref, skip_ref, q_ref, k_ref, v_ref, g_ref, out_hbm, gq_hbm, gk_hbm, gv_hbm,
    out, gq, gk, gv, conv_ref, back_ref, sems,
):
    batch, chans = q_ref.shape[0], q_ref.shape[1]
    span = chans // CHUNKS
    peers = span // own
    sent = []
    for n in range(CHUNKS):
        part = pl.ds(n * span, span)
        skip = skip_ref[part, :]
        for b in range(batch):
            conv, back = conv_ref.at[n * batch + b], back_ref.at[n * batch + b]
            for j in range(own):
                at = n * peers * rows + b * own + j
                conv[pl.ds(j, peers, stride=own), :] = r_ref[pl.ds(at, peers, stride=rows), :]
                at += batch * own
                back[pl.ds(j, peers, stride=own), :] = r_ref[pl.ds(at, peers, stride=rows), :]
            query, keys = q_ref[b, part].astype(F32), k_ref[b, part].astype(F32)
            values, upstream = v_ref[b, part].astype(F32), g_ref[b, part].astype(F32)
            gated = conv[...] + skip * (keys * values)
            total = back[...] + skip * (upstream * query)
            out[b, part] = (query * gated).astype(BF16)
            gq[b, part] = (upstream * gated).astype(BF16)
            gk[b, part] = (total * values).astype(BF16)
            gv[b, part] = (total * keys).astype(BF16)
        for i, (src, dst) in enumerate(((out, out_hbm), (gq, gq_hbm), (gk, gk_hbm), (gv, gv_hbm))):
            copy = pltpu.make_async_copy(src.at[:, part], dst.at[:, part], sems.at[4 * n + i])
            copy.start()
            sent.append(copy)
    for copy in sent:
        copy.wait()


def join_kernel(own, core_ref, mine_ref, other_ref, out_ref):
    peers = mine_ref.shape[0]
    for j in range(own):
        out_ref[pl.ds(j, peers, stride=own), :] = jnp.where(
            core_ref[0] == j, mine_ref[...], other_ref[...]
        )


VMEM = pl.BlockSpec(memory_space=pltpu.VMEM)
SMEM = pl.BlockSpec(memory_space=pltpu.SMEM)
HBM = pl.BlockSpec(memory_space=pltpu.HBM)
MIB = 1024 * 1024


def shards(devices, groups, tables, query_proj, key_proj, value_proj, long_filter, skip_gain, out_grad):
    batch, chans, cols = query_proj.shape
    peers = devices * groups
    own = chans // peers
    rows_in = 2 * batch * own + 1
    rows_out = rows_in
    core = lax.rem(lax.axis_index("dp"), own).astype(jnp.int32).reshape(1)

    def params(mib):
        return pltpu.CompilerParams(vmem_limit_bytes=mib * MIB)

    def exchange(flat, rows):
        shaped = flat.reshape(peers, rows, 1, cols)
        moved = lax.all_to_all(shaped, ("seq", "dp"), split_axis=0, concat_axis=0, tiled=True)
        return moved.reshape(peers * rows, cols)

    with jax.named_scope("pre"):
        wide = pltpu.VMEM((batch, chans, cols), BF16)
        send = pl.pallas_call(
            lambda *refs: pre_kernel(rows_in, own, *refs),
            out_shape=pltpu.VMEM((peers * rows_in, cols), F32),
            in_specs=[SMEM] + [HBM] * 5,
            out_specs=VMEM,
            scratch_shapes=[
                wide, wide, wide, wide,
                pltpu.VMEM((chans, cols), F32),
                pltpu.VMEM((2 * batch * CHUNKS, chans // CHUNKS, cols), F32),
                pltpu.SemaphoreType.DMA((5 * CHUNKS,)),
            ],
            compiler_params=params(56),
        )(core, query_proj, key_proj, value_proj, out_grad, long_filter)
    with jax.named_scope("gather"):
        arrived = exchange(send, rows_in)
    with jax.named_scope("mid"):
        send = pl.pallas_call(
            lambda *refs: mid_kernel(devices, groups, own, batch, rows_in, rows_out, *refs),
            out_shape=jax.ShapeDtypeStruct((peers * rows_out, cols), F32),
            in_specs=[VMEM] * (1 + len(tables)),
            out_specs=VMEM,
            compiler_params=params(48),
        )(arrived, *tables)
    with jax.named_scope("scatter"):
        shaped = send.reshape(peers, rows_out, 1, cols)
        returned = lax.all_to_all(shaped, ("seq", "dp"), split_axis=0, concat_axis=0, tiled=True)
    with jax.named_scope("swap"):
        mine = returned[:, rows_out - 1].reshape(peers, cols)
        pairs = [(d, d + 1 - 2 * (d % own)) for d in range(groups)]
        other = lax.ppermute(mine, "dp", pairs)
    with jax.named_scope("post"):
        plane = jax.ShapeDtypeStruct((batch, chans, cols), BF16)
        planes = pl.pallas_call(
            lambda *refs: post_kernel(rows_out, own, *refs),
            out_shape=[plane] * 4,
            in_specs=[VMEM] * 6,
            out_specs=[HBM] * 4,
            scratch_shapes=[wide] * 4
            + [pltpu.VMEM((batch * CHUNKS, chans // CHUNKS, cols), F32)] * 2
            + [pltpu.SemaphoreType.DMA((4 * CHUNKS,))],
            compiler_params=params(48),
            cost_estimate=pl.CostEstimate(flops=10**6, bytes_accessed=4 * 10**6, transcendentals=0),
        )(returned.reshape(peers * rows_out, cols), skip_gain[:, None], query_proj, key_proj, value_proj, out_grad)
    with jax.named_scope("join"):
        grad_filter = pl.pallas_call(
            lambda *refs: join_kernel(own, *refs),
            out_shape=jax.ShapeDtypeStruct((chans, cols), F32),
            in_specs=[SMEM, VMEM, VMEM],
            out_specs=VMEM,
            compiler_params=params(48),
            cost_estimate=pl.CostEstimate(flops=10**5, bytes_accessed=5 * 10**5, transcendentals=0),
        )(core, mine, other)
    return (*planes, grad_filter)


def solution(mesh):
    devices, groups = mesh.shape["seq"], mesh.shape["dp"]
    tables = build_tables(devices, 1.0 / math.sqrt(2 * groups * devices * LANES))

    def run(*args):
        return shards(devices, groups, tables, *args)

    wide = P("dp", None, "seq")
    return jax.shard_map(
        run,
        mesh=mesh,
        in_specs=(wide, wide, wide, P(None, "seq"), P(), wide),
        out_specs=(wide, wide, wide, wide, P(None, "seq")),
        check_vma=False,
    )
```

```python
import math

import jax
import jax.numpy as jnp
import numpy as np
from jax import lax
from jax.experimental import pallas as pl
from jax.experimental.pallas import tpu as pltpu
from jax.sharding import PartitionSpec as P

F32 = jnp.float32
BF16 = jnp.bfloat16
LANES = 128
CHUNKS = 4


def split_np(table):
    high = table.astype(jnp.bfloat16)
    low = (table - high.astype(np.float64)).astype(jnp.bfloat16)
    return high, low


def build_tables(half, scale):
    K1 = 2 * half
    total = K1 * LANES
    k1 = np.arange(K1)[:, None]
    n1 = np.arange(half)[None, :]
    ang = 2.0 * np.pi * ((k1 * n1) % K1) / K1
    c1, s1 = np.cos(ang), np.sin(ang)
    enter = np.block([[c1, s1], [-s1, c1]])
    enter_real = np.concatenate([c1, -s1], 0)
    n2 = np.arange(LANES)[:, None]
    k2 = np.arange(LANES)[None, :]
    ang2 = 2.0 * np.pi * ((n2 * k2) % LANES) / LANES
    c2, s2 = np.cos(ang2), np.sin(ang2)
    lane_fwd = np.block([[c2, -s2], [s2, c2]])
    lane_inv = np.block([[c2, s2], [-s2, c2]])
    leave = np.block([[c1.T, -s1.T], [s1.T, c1.T]]) / total
    leave_real = leave[:half] * scale
    phase = (np.arange(K1)[:, None] * np.arange(LANES)[None, :]) % total
    angt = 2.0 * np.pi * phase / total
    turn = np.concatenate([np.cos(angt), np.sin(angt)], 1).astype(np.float32)

    def left(table):
        high, low = split_np(table)
        return np.concatenate([high, high, low], 1)

    def right(table):
        high, low = split_np(table)
        return np.concatenate([high, high, low], 0)

    return (
        left(enter), left(enter_real), right(lane_fwd), right(lane_inv),
        left(leave), left(leave_real), turn,
    )


def parts(value, axis):
    high = value.astype(BF16)
    low = (value - high.astype(F32)).astype(BF16)
    return jnp.concatenate([high, low, high], axis)


def mm(a, b):
    return jnp.dot(a, b, preferred_element_type=F32)


def twist_forward(part, turn_cos, turn_sin):
    half = part.shape[0] // 2
    re, im = part[:half], part[half:]
    return jnp.concatenate(
        [re * turn_cos + im * turn_sin, im * turn_cos - re * turn_sin], 1
    )


def twist_back(part, turn_cos, turn_sin):
    re, im = part[:, :LANES], part[:, LANES:]
    return jnp.concatenate(
        [re * turn_cos - im * turn_sin, im * turn_cos + re * turn_sin], 0
    )


def pre_kernel(
    rows, own, core_ref, q_hbm, k_hbm, v_hbm, g_hbm, f_hbm, send, q, k, v, g, f, hold, sems
):
    batch, chans = q.shape[0], q.shape[1]
    peers = chans // own
    planes = ((k_hbm, k), (v_hbm, v), (g_hbm, g), (q_hbm, q), (f_hbm, f))
    copies = [
        pltpu.make_async_copy(src, dst, sems.at[i]) for i, (src, dst) in enumerate(planes)
    ]
    for copy in copies:
        copy.start()
    for sig, (left, right) in enumerate(((k, v), (g, q))):
        copies[2 * sig].wait()
        copies[2 * sig + 1].wait()
        for b in range(batch):
            slot = hold.at[sig * batch + b]
            slot[...] = left[b].astype(F32) * right[b].astype(F32)
            for j in range(own):
                send[pl.ds((sig * batch + b) * own + j, peers, stride=rows), :] = slot[
                    pl.ds(j, peers, stride=own), :
                ]
    copies[4].wait()
    row = f[pl.ds(0, peers, stride=own), :]
    for j in range(1, own):
        row = jnp.where(core_ref[0] == j, f[pl.ds(j, peers, stride=own), :], row)
    send[pl.ds(2 * batch * own, peers, stride=rows), :] = row


def leave_product(table, data):
    depth = data.shape[0]
    high = data.astype(BF16)
    low = (data - high.astype(F32)).astype(BF16)
    first = table[:, :depth]
    return mm(first, high) + mm(first, low) + mm(table[:, 2 * depth :], high)


def mid_kernel(
    devices, groups, own, batch, rows_in, rows_out, r_ref, enter, enter_real, lane_fwd, lane_inv,
    leave, leave_real, turn_ref, send_ref,
):
    turn_cos, turn_sin = turn_ref[:, :LANES], turn_ref[:, LANES:]
    K1 = 2 * devices
    step_in, step_out = groups * rows_in, groups * rows_out

    def lanes(value, i):
        return value[:, i * LANES : (i + 1) * LANES]

    def load(j, sig, d):
        base = d * rows_in + sig * batch * own + j
        re = r_ref[pl.ds(base, devices, stride=step_in), :]
        im = r_ref[pl.ds(base + own, devices, stride=step_in), :]
        return jnp.concatenate([re, im], 0)

    def forward(value, count):
        turned = [twist_forward(lanes(value, i), turn_cos, turn_sin) for i in range(count)]
        return mm(parts(jnp.concatenate(turned, 0), 1), lane_fwd[...])

    def inverse(spread, table, count):
        turned = [
            twist_back(spread[i * K1 : (i + 1) * K1], turn_cos, turn_sin) for i in range(count)
        ]
        return leave_product(table[...], jnp.concatenate(turned, 1))

    def pair(spec, i):
        rows = spec[i * K1 : (i + 1) * K1]
        return rows[:, :LANES], rows[:, LANES:]

    count = 2 * groups
    taps = [
        r_ref[pl.ds(j * rows_in + 2 * batch * own, devices, stride=step_in), :]
        for j in range(own)
    ]
    loaded = [
        jnp.concatenate([load(j, sig, d) for sig in range(2) for d in range(groups)], 1)
        for j in range(own)
    ]
    entered = [mm(enter[...], parts(value, 0)) for value in loaded]
    real = mm(enter_real[...], parts(jnp.concatenate(taps, 1), 0))
    taps_spec = forward(real, own)
    specs = [forward(value, count) for value in entered]
    spreads, crosses = [], []
    for j in range(own):
        hr, hi = pair(taps_spec, j)
        cross_re = cross_im = 0.0
        conv, back = [], []
        for d in range(groups):
            mr, mi = pair(specs[j], d)
            wr, wi = pair(specs[j], groups + d)
            conv.append(jnp.concatenate([mr * hr - mi * hi, mr * hi + mi * hr], 1))
            back.append(jnp.concatenate([wr * hr + wi * hi, wi * hr - wr * hi], 1))
            cross_re = cross_re + (wr * mr + wi * mi)
            cross_im = cross_im + (wi * mr - wr * mi)
        spreads.append(mm(parts(jnp.concatenate(conv + back, 0), 1), lane_inv[...]))
        crosses.append(jnp.concatenate([cross_re, cross_im], 1))
    cross_spread = mm(parts(jnp.concatenate(crosses, 0), 1), lane_inv[...])
    for j in range(own):
        final = inverse(spreads[j], leave, count)
        for sig in range(2):
            for d in range(groups):
                part = lanes(final, sig * groups + d)
                for b in range(batch):
                    base = d * rows_out + (sig * batch + b) * own + j
                    send_ref[pl.ds(base, devices, stride=step_out), :] = part[
                        b * devices : (b + 1) * devices
                    ]
    terms = inverse(cross_spread, leave_real, own)
    for j in range(own):
        for d in range(j, groups, own):
            base = d * rows_out + 2 * batch * own
            send_ref[pl.ds(base, devices, stride=step_out), :] = lanes(terms, j)


def post_kernel(
    rows, own, r_ref, skip_ref, q_ref, k_ref, v_ref, g_ref, out_hbm, gq_hbm, gk_hbm, gv_hbm,
    out, gq, gk, gv, conv_ref, back_ref, sems,
):
    batch, chans = q_ref.shape[0], q_ref.shape[1]
    span = chans // CHUNKS
    peers = span // own
    sent = []
    for n in range(CHUNKS):
        part = pl.ds(n * span, span)
        skip = jnp.broadcast_to(skip_ref[n : n + 1, :], (LANES, span)).T
        for b in range(batch):
            conv, back = conv_ref.at[n * batch + b], back_ref.at[n * batch + b]
            for j in range(own):
                at = n * peers * rows + b * own + j
                conv[pl.ds(j, peers, stride=own), :] = r_ref[pl.ds(at, peers, stride=rows), :]
                at += batch * own
                back[pl.ds(j, peers, stride=own), :] = r_ref[pl.ds(at, peers, stride=rows), :]
            query, keys = q_ref[b, part].astype(F32), k_ref[b, part].astype(F32)
            values, upstream = v_ref[b, part].astype(F32), g_ref[b, part].astype(F32)
            gated = conv[...] + skip * (keys * values)
            total = back[...] + skip * (upstream * query)
            out[b, part] = (query * gated).astype(BF16)
            gq[b, part] = (upstream * gated).astype(BF16)
            gk[b, part] = (total * values).astype(BF16)
            gv[b, part] = (total * keys).astype(BF16)
        for i, (src, dst) in enumerate(((out, out_hbm), (gq, gq_hbm), (gk, gk_hbm), (gv, gv_hbm))):
            copy = pltpu.make_async_copy(src.at[:, part], dst.at[:, part], sems.at[4 * n + i])
            copy.start()
            sent.append(copy)
    for copy in sent:
        copy.wait()


def join_kernel(own, core_ref, mine_ref, other_ref, out_ref):
    peers = mine_ref.shape[0]
    for j in range(own):
        out_ref[pl.ds(j, peers, stride=own), :] = jnp.where(
            core_ref[0] == j, mine_ref[...], other_ref[...]
        )


VMEM = pl.BlockSpec(memory_space=pltpu.VMEM)
SMEM = pl.BlockSpec(memory_space=pltpu.SMEM)
HBM = pl.BlockSpec(memory_space=pltpu.HBM)
MIB = 1024 * 1024


def shards(devices, groups, tables, query_proj, key_proj, value_proj, long_filter, skip_gain, out_grad):
    batch, chans, cols = query_proj.shape
    peers = devices * groups
    own = chans // peers
    rows_in = 2 * batch * own + 1
    rows_out = rows_in
    core = lax.rem(lax.axis_index("dp"), own).astype(jnp.int32).reshape(1)

    def params(mib):
        return pltpu.CompilerParams(vmem_limit_bytes=mib * MIB)

    def exchange(flat, rows):
        shaped = flat.reshape(peers, rows, 1, cols)
        moved = lax.all_to_all(shaped, ("seq", "dp"), split_axis=0, concat_axis=0, tiled=True)
        return moved.reshape(peers * rows, cols)

    with jax.named_scope("pre"):
        wide = pltpu.VMEM((batch, chans, cols), BF16)
        send = pl.pallas_call(
            lambda *refs: pre_kernel(rows_in, own, *refs),
            out_shape=pltpu.VMEM((peers * rows_in, cols), F32),
            in_specs=[SMEM] + [HBM] * 5,
            out_specs=VMEM,
            scratch_shapes=[
                wide, wide, wide, wide,
                pltpu.VMEM((chans, cols), F32),
                pltpu.VMEM((2 * batch, chans, cols), F32),
                pltpu.SemaphoreType.DMA((5,)),
            ],
            compiler_params=params(56),
        )(core, query_proj, key_proj, value_proj, out_grad, long_filter)
    with jax.named_scope("gather"):
        arrived = exchange(send, rows_in)
    with jax.named_scope("mid"):
        send = pl.pallas_call(
            lambda *refs: mid_kernel(devices, groups, own, batch, rows_in, rows_out, *refs),
            out_shape=jax.ShapeDtypeStruct((peers * rows_out, cols), F32),
            in_specs=[VMEM] * (1 + len(tables)),
            out_specs=VMEM,
            compiler_params=params(48),
        )(arrived, *tables)
    with jax.named_scope("scatter"):
        shaped = send.reshape(peers, rows_out, 1, cols)
        returned = lax.all_to_all(shaped, ("seq", "dp"), split_axis=0, concat_axis=0, tiled=True)
    with jax.named_scope("swap"):
        mine = returned[:, rows_out - 1].reshape(peers, cols)
        pairs = [(d, d + 1 - 2 * (d % own)) for d in range(groups)]
        other = lax.ppermute(mine, "dp", pairs)
    with jax.named_scope("post"):
        plane = jax.ShapeDtypeStruct((batch, chans, cols), BF16)
        planes = pl.pallas_call(
            lambda *refs: post_kernel(rows_out, own, *refs),
            out_shape=[plane] * 4,
            in_specs=[VMEM] * 6,
            out_specs=[HBM] * 4,
            scratch_shapes=[wide] * 4
            + [pltpu.VMEM((batch * CHUNKS, chans // CHUNKS, cols), F32)] * 2
            + [pltpu.SemaphoreType.DMA((4 * CHUNKS,))],
            compiler_params=params(48),
            cost_estimate=pl.CostEstimate(flops=10**6, bytes_accessed=4 * 10**6, transcendentals=0),
        )(returned.reshape(peers * rows_out, cols), skip_gain.reshape(CHUNKS, chans // CHUNKS), query_proj, key_proj, value_proj, out_grad)
    with jax.named_scope("join"):
        grad_filter = pl.pallas_call(
            lambda *refs: join_kernel(own, *refs),
            out_shape=jax.ShapeDtypeStruct((chans, cols), F32),
            in_specs=[SMEM, VMEM, VMEM],
            out_specs=VMEM,
            compiler_params=params(48),
            cost_estimate=pl.CostEstimate(flops=10**5, bytes_accessed=5 * 10**5, transcendentals=0),
        )(core, mine, other)
    return (*planes, grad_filter)


def solution(mesh):
    devices, groups = mesh.shape["seq"], mesh.shape["dp"]
    tables = build_tables(devices, 1.0 / math.sqrt(2 * groups * devices * LANES))

    def run(*args):
        return shards(devices, groups, tables, *args)

    wide = P("dp", None, "seq")
    return jax.shard_map(
        run,
        mesh=mesh,
        in_specs=(wide, wide, wide, P(None, "seq"), P(), wide),
        out_specs=(wide, wide, wide, wide, P(None, "seq")),
        check_vma=False,
    )
```

```python
import math

import jax
import jax.numpy as jnp
import numpy as np
from jax import lax
from jax.experimental import pallas as pl
from jax.experimental.pallas import tpu as pltpu
from jax.sharding import PartitionSpec as P

F32 = jnp.float32
BF16 = jnp.bfloat16
LANES = 128
CHUNKS = 2


def split_np(table):
    high = table.astype(jnp.bfloat16)
    low = (table - high.astype(np.float64)).astype(jnp.bfloat16)
    return high, low


def build_tables(half, scale):
    K1 = 2 * half
    total = K1 * LANES
    k1 = np.arange(K1)[:, None]
    n1 = np.arange(half)[None, :]
    ang = 2.0 * np.pi * ((k1 * n1) % K1) / K1
    c1, s1 = np.cos(ang), np.sin(ang)
    enter = np.block([[c1, s1], [-s1, c1]])
    enter_real = np.concatenate([c1, -s1], 0)
    n2 = np.arange(LANES)[:, None]
    k2 = np.arange(LANES)[None, :]
    ang2 = 2.0 * np.pi * ((n2 * k2) % LANES) / LANES
    c2, s2 = np.cos(ang2), np.sin(ang2)
    lane_fwd = np.block([[c2, -s2], [s2, c2]])
    lane_inv = np.block([[c2, s2], [-s2, c2]])
    leave = np.block([[c1.T, -s1.T], [s1.T, c1.T]]) / total
    leave_real = leave[:half] * scale
    phase = (np.arange(K1)[:, None] * np.arange(LANES)[None, :]) % total
    angt = 2.0 * np.pi * phase / total
    turn = np.concatenate([np.cos(angt), np.sin(angt)], 1).astype(np.float32)

    def left(table):
        high, low = split_np(table)
        return np.concatenate([high, high, low], 1)

    def right(table):
        high, low = split_np(table)
        return np.concatenate([high, high, low], 0)

    return (
        left(enter), left(enter_real), right(lane_fwd), right(lane_inv),
        left(leave), left(leave_real), turn,
    )


def parts(value, axis):
    high = value.astype(BF16)
    low = (value - high.astype(F32)).astype(BF16)
    return jnp.concatenate([high, low, high], axis)


def mm(a, b):
    return jnp.dot(a, b, preferred_element_type=F32)


def twist_forward(part, turn_cos, turn_sin):
    half = part.shape[0] // 2
    re, im = part[:half], part[half:]
    return jnp.concatenate(
        [re * turn_cos + im * turn_sin, im * turn_cos - re * turn_sin], 1
    )


def twist_back(part, turn_cos, turn_sin):
    re, im = part[:, :LANES], part[:, LANES:]
    return jnp.concatenate(
        [re * turn_cos - im * turn_sin, im * turn_cos + re * turn_sin], 0
    )


def pre_kernel(
    rows, own, core_ref, q_hbm, k_hbm, v_hbm, g_hbm, f_hbm, send, q, k, v, g, f, hold, sems
):
    batch, chans = q.shape[0], q.shape[1]
    peers = chans // own
    planes = ((k_hbm, k), (v_hbm, v), (g_hbm, g), (q_hbm, q), (f_hbm, f))
    copies = [
        pltpu.make_async_copy(src, dst, sems.at[i]) for i, (src, dst) in enumerate(planes)
    ]
    for copy in copies:
        copy.start()
    for sig, (left, right) in enumerate(((k, v), (g, q))):
        copies[2 * sig].wait()
        copies[2 * sig + 1].wait()
        for b in range(batch):
            slot = hold.at[sig * batch + b]
            slot[...] = left[b].astype(F32) * right[b].astype(F32)
            for j in range(own):
                send[pl.ds((sig * batch + b) * own + j, peers, stride=rows), :] = slot[
                    pl.ds(j, peers, stride=own), :
                ]
    copies[4].wait()
    row = f[pl.ds(0, peers, stride=own), :]
    for j in range(1, own):
        row = jnp.where(core_ref[0] == j, f[pl.ds(j, peers, stride=own), :], row)
    send[pl.ds(2 * batch * own, peers, stride=rows), :] = row


def leave_product(table, data):
    depth = data.shape[0]
    high = data.astype(BF16)
    low = (data - high.astype(F32)).astype(BF16)
    first = table[:, :depth]
    return mm(first, high) + mm(first, low) + mm(table[:, 2 * depth :], high)


def mid_kernel(
    devices, groups, own, batch, rows_in, rows_out, r_ref, enter, enter_real, lane_fwd, lane_inv,
    leave, leave_real, turn_ref, send_ref,
):
    turn_cos, turn_sin = turn_ref[:, :LANES], turn_ref[:, LANES:]
    K1 = 2 * devices
    step_in, step_out = groups * rows_in, groups * rows_out

    def lanes(value, i):
        return value[:, i * LANES : (i + 1) * LANES]

    def load(j, sig, d):
        base = d * rows_in + sig * batch * own + j
        re = r_ref[pl.ds(base, devices, stride=step_in), :]
        im = r_ref[pl.ds(base + own, devices, stride=step_in), :]
        return jnp.concatenate([re, im], 0)

    def forward(value, count):
        turned = [twist_forward(lanes(value, i), turn_cos, turn_sin) for i in range(count)]
        return mm(parts(jnp.concatenate(turned, 0), 1), lane_fwd[...])

    def inverse(spread, table, count):
        turned = [
            twist_back(spread[i * K1 : (i + 1) * K1], turn_cos, turn_sin) for i in range(count)
        ]
        return leave_product(table[...], jnp.concatenate(turned, 1))

    def pair(spec, i):
        rows = spec[i * K1 : (i + 1) * K1]
        return rows[:, :LANES], rows[:, LANES:]

    count = 2 * groups
    taps = [
        r_ref[pl.ds(j * rows_in + 2 * batch * own, devices, stride=step_in), :]
        for j in range(own)
    ]
    loaded = [
        jnp.concatenate([load(j, sig, d) for sig in range(2) for d in range(groups)], 1)
        for j in range(own)
    ]
    entered = [mm(enter[...], parts(value, 0)) for value in loaded]
    real = mm(enter_real[...], parts(jnp.concatenate(taps, 1), 0))
    taps_spec = forward(real, own)
    specs = [forward(value, count) for value in entered]
    spreads, crosses = [], []
    for j in range(own):
        hr, hi = pair(taps_spec, j)
        cross_re = cross_im = 0.0
        conv, back = [], []
        for d in range(groups):
            mr, mi = pair(specs[j], d)
            wr, wi = pair(specs[j], groups + d)
            conv.append(jnp.concatenate([mr * hr - mi * hi, mr * hi + mi * hr], 1))
            back.append(jnp.concatenate([wr * hr + wi * hi, wi * hr - wr * hi], 1))
            cross_re = cross_re + (wr * mr + wi * mi)
            cross_im = cross_im + (wi * mr - wr * mi)
        spreads.append(mm(parts(jnp.concatenate(conv + back, 0), 1), lane_inv[...]))
        crosses.append(jnp.concatenate([cross_re, cross_im], 1))
    cross_spread = mm(parts(jnp.concatenate(crosses, 0), 1), lane_inv[...])
    for j in range(own):
        final = inverse(spreads[j], leave, count)
        for sig in range(2):
            for d in range(groups):
                part = lanes(final, sig * groups + d)
                for b in range(batch):
                    base = d * rows_out + (sig * batch + b) * own + j
                    send_ref[pl.ds(base, devices, stride=step_out), :] = part[
                        b * devices : (b + 1) * devices
                    ]
    terms = inverse(cross_spread, leave_real, own)
    for j in range(own):
        for d in range(j, groups, own):
            base = d * rows_out + 2 * batch * own
            send_ref[pl.ds(base, devices, stride=step_out), :] = lanes(terms, j)


def post_kernel(
    rows, own, r_ref, skip_ref, q_ref, k_ref, v_ref, g_ref, out_hbm, gq_hbm, gk_hbm, gv_hbm,
    out, gq, gk, gv, conv_ref, back_ref, sems,
):
    batch, chans = q_ref.shape[0], q_ref.shape[1]
    span = chans // CHUNKS
    peers = span // own
    sent = []
    for n in range(CHUNKS):
        part = pl.ds(n * span, span)
        skip = jnp.broadcast_to(skip_ref[n : n + 1, :], (LANES, span)).T
        for b in range(batch):
            conv, back = conv_ref.at[n * batch + b], back_ref.at[n * batch + b]
            for j in range(own):
                at = n * peers * rows + b * own + j
                conv[pl.ds(j, peers, stride=own), :] = r_ref[pl.ds(at, peers, stride=rows), :]
                at += batch * own
                back[pl.ds(j, peers, stride=own), :] = r_ref[pl.ds(at, peers, stride=rows), :]
            query, keys = q_ref[b, part].astype(F32), k_ref[b, part].astype(F32)
            values, upstream = v_ref[b, part].astype(F32), g_ref[b, part].astype(F32)
            gated = conv[...] + skip * (keys * values)
            total = back[...] + skip * (upstream * query)
            out[b, part] = (query * gated).astype(BF16)
            gq[b, part] = (upstream * gated).astype(BF16)
            gk[b, part] = (total * values).astype(BF16)
            gv[b, part] = (total * keys).astype(BF16)
        for i, (src, dst) in enumerate(((out, out_hbm), (gq, gq_hbm), (gk, gk_hbm), (gv, gv_hbm))):
            copy = pltpu.make_async_copy(src.at[:, part], dst.at[:, part], sems.at[4 * n + i])
            copy.start()
            sent.append(copy)
    for copy in sent:
        copy.wait()


def join_kernel(own, core_ref, mine_ref, other_ref, out_ref):
    peers = mine_ref.shape[0]
    for j in range(own):
        out_ref[pl.ds(j, peers, stride=own), :] = jnp.where(
            core_ref[0] == j, mine_ref[...], other_ref[...]
        )


VMEM = pl.BlockSpec(memory_space=pltpu.VMEM)
SMEM = pl.BlockSpec(memory_space=pltpu.SMEM)
HBM = pl.BlockSpec(memory_space=pltpu.HBM)
MIB = 1024 * 1024


def shards(devices, groups, tables, query_proj, key_proj, value_proj, long_filter, skip_gain, out_grad):
    batch, chans, cols = query_proj.shape
    peers = devices * groups
    own = chans // peers
    rows_in = 2 * batch * own + 1
    rows_out = rows_in
    core = lax.rem(lax.axis_index("dp"), own).astype(jnp.int32).reshape(1)

    def params(mib):
        return pltpu.CompilerParams(vmem_limit_bytes=mib * MIB)

    def exchange(flat, rows):
        shaped = flat.reshape(peers, rows, 1, cols)
        moved = lax.all_to_all(shaped, ("seq", "dp"), split_axis=0, concat_axis=0, tiled=True)
        return moved.reshape(peers * rows, cols)

    with jax.named_scope("pre"):
        wide = pltpu.VMEM((batch, chans, cols), BF16)
        send = pl.pallas_call(
            lambda *refs: pre_kernel(rows_in, own, *refs),
            out_shape=pltpu.VMEM((peers * rows_in, cols), F32),
            in_specs=[SMEM] + [HBM] * 5,
            out_specs=VMEM,
            scratch_shapes=[
                wide, wide, wide, wide,
                pltpu.VMEM((chans, cols), F32),
                pltpu.VMEM((2 * batch, chans, cols), F32),
                pltpu.SemaphoreType.DMA((5,)),
            ],
            compiler_params=params(56),
        )(core, query_proj, key_proj, value_proj, out_grad, long_filter)
    with jax.named_scope("gather"):
        arrived = exchange(send, rows_in)
    with jax.named_scope("mid"):
        send = pl.pallas_call(
            lambda *refs: mid_kernel(devices, groups, own, batch, rows_in, rows_out, *refs),
            out_shape=jax.ShapeDtypeStruct((peers * rows_out, cols), F32),
            in_specs=[VMEM] * (1 + len(tables)),
            out_specs=VMEM,
            compiler_params=params(48),
        )(arrived, *tables)
    with jax.named_scope("scatter"):
        shaped = send.reshape(peers, rows_out, 1, cols)
        returned = lax.all_to_all(shaped, ("seq", "dp"), split_axis=0, concat_axis=0, tiled=True)
    with jax.named_scope("swap"):
        mine = returned[:, rows_out - 1].reshape(peers, cols)
        pairs = [(d, d + 1 - 2 * (d % own)) for d in range(groups)]
        other = lax.ppermute(mine, "dp", pairs)
    with jax.named_scope("post"):
        plane = jax.ShapeDtypeStruct((batch, chans, cols), BF16)
        planes = pl.pallas_call(
            lambda *refs: post_kernel(rows_out, own, *refs),
            out_shape=[plane] * 4,
            in_specs=[VMEM] * 6,
            out_specs=[HBM] * 4,
            scratch_shapes=[wide] * 4
            + [pltpu.VMEM((batch * CHUNKS, chans // CHUNKS, cols), F32)] * 2
            + [pltpu.SemaphoreType.DMA((4 * CHUNKS,))],
            compiler_params=params(48),
            cost_estimate=pl.CostEstimate(flops=10**6, bytes_accessed=4 * 10**6, transcendentals=0),
        )(returned.reshape(peers * rows_out, cols), skip_gain.reshape(CHUNKS, chans // CHUNKS), query_proj, key_proj, value_proj, out_grad)
    with jax.named_scope("join"):
        grad_filter = pl.pallas_call(
            lambda *refs: join_kernel(own, *refs),
            out_shape=jax.ShapeDtypeStruct((chans, cols), F32),
            in_specs=[SMEM, VMEM, VMEM],
            out_specs=VMEM,
            compiler_params=params(48),
            cost_estimate=pl.CostEstimate(flops=10**5, bytes_accessed=5 * 10**5, transcendentals=0),
        )(core, mine, other)
    return (*planes, grad_filter)


def solution(mesh):
    devices, groups = mesh.shape["seq"], mesh.shape["dp"]
    tables = build_tables(devices, 1.0 / math.sqrt(2 * groups * devices * LANES))

    def run(*args):
        return shards(devices, groups, tables, *args)

    wide = P("dp", None, "seq")
    return jax.shard_map(
        run,
        mesh=mesh,
        in_specs=(wide, wide, wide, P(None, "seq"), P(), wide),
        out_specs=(wide, wide, wide, wide, P(None, "seq")),
        check_vma=False,
    )
```

```python
import math

import jax
import jax.numpy as jnp
import numpy as np
from jax import lax
from jax.experimental import pallas as pl
from jax.experimental.pallas import tpu as pltpu
from jax.sharding import PartitionSpec as P

F32 = jnp.float32
BF16 = jnp.bfloat16
LANES = 128
CHUNKS = 2


def split_np(table):
    high = table.astype(jnp.bfloat16)
    low = (table - high.astype(np.float64)).astype(jnp.bfloat16)
    return high, low


def build_tables(half, scale):
    K1 = 2 * half
    total = K1 * LANES
    k1 = np.arange(K1)[:, None]
    n1 = np.arange(half)[None, :]
    ang = 2.0 * np.pi * ((k1 * n1) % K1) / K1
    c1, s1 = np.cos(ang), np.sin(ang)
    enter = np.block([[c1, s1], [-s1, c1]])
    enter_real = np.concatenate([c1, -s1], 0)
    n2 = np.arange(LANES)[:, None]
    k2 = np.arange(LANES)[None, :]
    ang2 = 2.0 * np.pi * ((n2 * k2) % LANES) / LANES
    c2, s2 = np.cos(ang2), np.sin(ang2)
    lane_fwd = np.block([[c2, -s2], [s2, c2]])
    lane_inv = np.block([[c2, s2], [-s2, c2]])
    leave = np.block([[c1.T, -s1.T], [s1.T, c1.T]]) / total
    leave_real = leave[:half] * scale
    phase = (np.arange(K1)[:, None] * np.arange(LANES)[None, :]) % total
    angt = 2.0 * np.pi * phase / total
    turn = np.concatenate([np.cos(angt), np.sin(angt)], 1).astype(np.float32)

    def left(table):
        high, low = split_np(table)
        return np.concatenate([high, high, low], 1)

    def right(table):
        high, low = split_np(table)
        return np.concatenate([high, high, low], 0)

    return (
        left(enter), left(enter_real), right(lane_fwd), right(lane_inv),
        left(leave), left(leave_real), turn,
    )


def parts(value, axis):
    high = value.astype(BF16)
    low = (value - high.astype(F32)).astype(BF16)
    return jnp.concatenate([high, low, high], axis)


def mm(a, b):
    return jnp.dot(a, b, preferred_element_type=F32)


def twist_forward(part, turn_cos, turn_sin):
    half = part.shape[0] // 2
    re, im = part[:half], part[half:]
    return jnp.concatenate(
        [re * turn_cos + im * turn_sin, im * turn_cos - re * turn_sin], 1
    )


def twist_back(part, turn_cos, turn_sin):
    re, im = part[:, :LANES], part[:, LANES:]
    return jnp.concatenate(
        [re * turn_cos - im * turn_sin, im * turn_cos + re * turn_sin], 0
    )


def pre_kernel(
    rows, own, core_ref, q_hbm, k_hbm, v_hbm, g_hbm, f_hbm, send, q, k, v, g, f, hold, sems
):
    batch, chans = q.shape[0], q.shape[1]
    peers = chans // own
    planes = ((k_hbm, k), (v_hbm, v), (g_hbm, g), (q_hbm, q), (f_hbm, f))
    copies = [
        pltpu.make_async_copy(src, dst, sems.at[i]) for i, (src, dst) in enumerate(planes)
    ]
    for copy in copies:
        copy.start()
    for sig, (left, right) in enumerate(((k, v), (g, q))):
        copies[2 * sig].wait()
        copies[2 * sig + 1].wait()
        for b in range(batch):
            slot = hold.at[sig * batch + b]
            slot[...] = left[b].astype(F32) * right[b].astype(F32)
            for j in range(own):
                send[pl.ds((sig * batch + b) * own + j, peers, stride=rows), :] = slot[
                    pl.ds(j, peers, stride=own), :
                ]
    copies[4].wait()
    row = f[pl.ds(0, peers, stride=own), :]
    for j in range(1, own):
        row = jnp.where(core_ref[0] == j, f[pl.ds(j, peers, stride=own), :], row)
    send[pl.ds(2 * batch * own, peers, stride=rows), :] = row


def mid_kernel(
    devices, groups, own, batch, rows_in, rows_out, r_ref, enter, enter_real, lane_fwd, lane_inv,
    leave, leave_real, turn_ref, send_ref,
):
    turn_cos, turn_sin = turn_ref[:, :LANES], turn_ref[:, LANES:]
    K1 = 2 * devices
    step_in, step_out = groups * rows_in, groups * rows_out

    def lanes(value, i):
        return value[:, i * LANES : (i + 1) * LANES]

    def load(j, sig, d):
        base = d * rows_in + sig * batch * own + j
        re = r_ref[pl.ds(base, devices, stride=step_in), :]
        im = r_ref[pl.ds(base + own, devices, stride=step_in), :]
        return jnp.concatenate([re, im], 0)

    def forward(value, count):
        turned = [twist_forward(lanes(value, i), turn_cos, turn_sin) for i in range(count)]
        return mm(parts(jnp.concatenate(turned, 0), 1), lane_fwd[...])

    def inverse(spread, table, count):
        turned = [
            twist_back(spread[i * K1 : (i + 1) * K1], turn_cos, turn_sin) for i in range(count)
        ]
        return mm(table[...], parts(jnp.concatenate(turned, 1), 0))

    def pair(spec, i):
        rows = spec[i * K1 : (i + 1) * K1]
        return rows[:, :LANES], rows[:, LANES:]

    count = 2 * groups
    taps = [
        r_ref[pl.ds(j * rows_in + 2 * batch * own, devices, stride=step_in), :]
        for j in range(own)
    ]
    loaded = [
        jnp.concatenate([load(j, sig, d) for sig in range(2) for d in range(groups)], 1)
        for j in range(own)
    ]
    entered = [mm(enter[...], parts(value, 0)) for value in loaded]
    real = mm(enter_real[...], parts(jnp.concatenate(taps, 1), 0))
    taps_spec = forward(real, own)
    specs = [forward(value, count) for value in entered]
    spreads, crosses = [], []
    for j in range(own):
        hr, hi = pair(taps_spec, j)
        cross_re = cross_im = 0.0
        conv, back = [], []
        for d in range(groups):
            mr, mi = pair(specs[j], d)
            wr, wi = pair(specs[j], groups + d)
            conv.append(jnp.concatenate([mr * hr - mi * hi, mr * hi + mi * hr], 1))
            back.append(jnp.concatenate([wr * hr + wi * hi, wi * hr - wr * hi], 1))
            cross_re = cross_re + (wr * mr + wi * mi)
            cross_im = cross_im + (wi * mr - wr * mi)
        spreads.append(mm(parts(jnp.concatenate(conv + back, 0), 1), lane_inv[...]))
        crosses.append(jnp.concatenate([cross_re, cross_im], 1))
    cross_spread = mm(parts(jnp.concatenate(crosses, 0), 1), lane_inv[...])
    for j in range(own):
        final = inverse(spreads[j], leave, count)
        for sig in range(2):
            for d in range(groups):
                part = lanes(final, sig * groups + d)
                for b in range(batch):
                    base = d * rows_out + (sig * batch + b) * own + j
                    send_ref[pl.ds(base, devices, stride=step_out), :] = part[
                        b * devices : (b + 1) * devices
                    ]
    terms = inverse(cross_spread, leave_real, own)
    for j in range(own):
        for d in range(j, groups, own):
            base = d * rows_out + 2 * batch * own
            send_ref[pl.ds(base, devices, stride=step_out), :] = lanes(terms, j)


def post_kernel(
    rows, own, r_ref, skip_ref, q_ref, k_ref, v_ref, g_ref, out_hbm, gq_hbm, gk_hbm, gv_hbm,
    out, gq, gk, gv, conv_ref, back_ref, sems,
):
    batch, chans = q_ref.shape[0], q_ref.shape[1]
    span = chans // CHUNKS
    peers = span // own
    sent = []
    for n in range(CHUNKS):
        part = pl.ds(n * span, span)
        skip = jnp.broadcast_to(skip_ref[n : n + 1, :], (LANES, span)).T
        for b in range(batch):
            conv, back = conv_ref.at[n * batch + b], back_ref.at[n * batch + b]
            for j in range(own):
                at = n * peers * rows + b * own + j
                conv[pl.ds(j, peers, stride=own), :] = r_ref[pl.ds(at, peers, stride=rows), :]
                at += batch * own
                back[pl.ds(j, peers, stride=own), :] = r_ref[pl.ds(at, peers, stride=rows), :]
            query, keys = q_ref[b, part].astype(F32), k_ref[b, part].astype(F32)
            values, upstream = v_ref[b, part].astype(F32), g_ref[b, part].astype(F32)
            gated = conv[...] + skip * (keys * values)
            total = back[...] + skip * (upstream * query)
            out[b, part] = (query * gated).astype(BF16)
            gq[b, part] = (upstream * gated).astype(BF16)
            gk[b, part] = (total * values).astype(BF16)
            gv[b, part] = (total * keys).astype(BF16)
        for i, (src, dst) in enumerate(((out, out_hbm), (gq, gq_hbm), (gk, gk_hbm), (gv, gv_hbm))):
            copy = pltpu.make_async_copy(src.at[:, part], dst.at[:, part], sems.at[4 * n + i])
            copy.start()
            sent.append(copy)
    for copy in sent:
        copy.wait()


def join_kernel(own, core_ref, mine_ref, other_ref, out_ref):
    peers = mine_ref.shape[0]
    for j in range(own):
        out_ref[pl.ds(j, peers, stride=own), :] = jnp.where(
            core_ref[0] == j, mine_ref[...], other_ref[...]
        )


VMEM = pl.BlockSpec(memory_space=pltpu.VMEM)
SMEM = pl.BlockSpec(memory_space=pltpu.SMEM)
HBM = pl.BlockSpec(memory_space=pltpu.HBM)
MIB = 1024 * 1024


def shards(devices, groups, tables, query_proj, key_proj, value_proj, long_filter, skip_gain, out_grad):
    batch, chans, cols = query_proj.shape
    peers = devices * groups
    own = chans // peers
    rows_in = 2 * batch * own + 1
    rows_out = rows_in
    core = lax.rem(lax.axis_index("dp"), own).astype(jnp.int32).reshape(1)

    def params(mib):
        return pltpu.CompilerParams(vmem_limit_bytes=mib * MIB)

    def exchange(flat, rows):
        shaped = flat.reshape(peers, rows, 1, cols)
        moved = lax.all_to_all(shaped, ("seq", "dp"), split_axis=0, concat_axis=0, tiled=True)
        return moved.reshape(peers * rows, cols)

    with jax.named_scope("pre"):
        wide = pltpu.VMEM((batch, chans, cols), BF16)
        send = pl.pallas_call(
            lambda *refs: pre_kernel(rows_in, own, *refs),
            out_shape=pltpu.VMEM((peers * rows_in, cols), F32),
            in_specs=[SMEM] + [HBM] * 5,
            out_specs=VMEM,
            scratch_shapes=[
                wide, wide, wide, wide,
                pltpu.VMEM((chans, cols), F32),
                pltpu.VMEM((2 * batch, chans, cols), F32),
                pltpu.SemaphoreType.DMA((5,)),
            ],
            compiler_params=params(56),
        )(core, query_proj, key_proj, value_proj, out_grad, long_filter)
    with jax.named_scope("gather"):
        arrived = exchange(send, rows_in)
    with jax.named_scope("mid"):
        send = pl.pallas_call(
            lambda *refs: mid_kernel(devices, groups, own, batch, rows_in, rows_out, *refs),
            out_shape=jax.ShapeDtypeStruct((peers * rows_out, cols), F32),
            in_specs=[VMEM] * (1 + len(tables)),
            out_specs=VMEM,
            compiler_params=params(48),
        )(arrived, *tables)
    with jax.named_scope("scatter"):
        shaped = send.reshape(peers, rows_out, 1, cols)
        returned = lax.all_to_all(shaped, ("seq", "dp"), split_axis=0, concat_axis=0, tiled=True)
    with jax.named_scope("swap"):
        mine = returned[:, rows_out - 1].reshape(peers, cols)
        pairs = [(d, d + 1 - 2 * (d % own)) for d in range(groups)]
        other = lax.ppermute(mine, "dp", pairs)
    with jax.named_scope("post"):
        plane = jax.ShapeDtypeStruct((batch, chans, cols), BF16)
        planes = pl.pallas_call(
            lambda *refs: post_kernel(rows_out, own, *refs),
            out_shape=[plane] * 4,
            in_specs=[VMEM] * 6,
            out_specs=[HBM] * 4,
            scratch_shapes=[wide] * 4
            + [pltpu.VMEM((batch * CHUNKS, chans // CHUNKS, cols), F32)] * 2
            + [pltpu.SemaphoreType.DMA((4 * CHUNKS,))],
            compiler_params=params(48),
            cost_estimate=pl.CostEstimate(flops=10**6, bytes_accessed=4 * 10**6, transcendentals=0),
        )(returned.reshape(peers * rows_out, cols), skip_gain.reshape(CHUNKS, chans // CHUNKS), query_proj, key_proj, value_proj, out_grad)
    with jax.named_scope("join"):
        grad_filter = pl.pallas_call(
            lambda *refs: join_kernel(own, *refs),
            out_shape=jax.ShapeDtypeStruct((chans, cols), F32),
            in_specs=[SMEM, VMEM, VMEM],
            out_specs=VMEM,
            compiler_params=params(48),
            cost_estimate=pl.CostEstimate(flops=10**5, bytes_accessed=5 * 10**5, transcendentals=0),
        )(core, mine, other)
    return (*planes, grad_filter)


def solution(mesh):
    devices, groups = mesh.shape["seq"], mesh.shape["dp"]
    tables = build_tables(devices, 1.0 / math.sqrt(2 * groups * devices * LANES))

    def run(*args):
        return shards(devices, groups, tables, *args)

    wide = P("dp", None, "seq")
    return jax.shard_map(
        run,
        mesh=mesh,
        in_specs=(wide, wide, wide, P(None, "seq"), P(), wide),
        out_specs=(wide, wide, wide, wide, P(None, "seq")),
        check_vma=False,
    )
```
